128 devices in a mesh: band: 16 (over y, z), patch: 8 (over x, core).
Axes of the slice: x: 4, y: 4, z: 4, core: 2. Of those that a mesh axis runs over, the one named last changes fastest.
Arguments:
- grid_state: bfloat16 [64, 2048, 512], P('band', 'patch'), may hold values from -6 to 6
- mesh_state: bfloat16 [16, 8, 256, 512], P('band', 'patch'), may hold values from -6 to 6
- g2m_features: bfloat16 [16, 8, 2048, 512], P('band', 'patch'), may hold values from -6 to 6
- g2m_sender: int32 [16, 8, 2048], P('band', 'patch'), may hold values from 0 to 2079, as said below
- g2m_receiver: int32 [16, 8, 2048], P('band', 'patch'), may hold values from 0 to 255
- g2m_blocks: int32 [16, 8], replicated, may hold values from 4 to 16, as said below
- proc_features: bfloat16 [16, 8, 2048, 512], P('band', 'patch'), may hold values from -6 to 6
- proc_sender: int32 [16, 8, 2048], P('band', 'patch'), may hold values from 0 to 4351, as said below
- proc_receiver: int32 [16, 8, 2048], P('band', 'patch'), may hold values from 0 to 255
- dec_features: bfloat16 [3, 64, 2048, 512], P(None, 'band', 'patch'), may hold values from -6 to 6
- dec_sender: int32 [3, 64, 2048], P(None, 'band', 'patch'), may hold values from 0 to 2111, as said below
- enc_weights: bfloat16 [9, 512, 512], replicated, may hold values from -0.25 to 0.25
- proc_weights: bfloat16 [7, 512, 512], replicated, may hold values from -0.25 to 0.25
- dec_weights: bfloat16 [7, 512, 512], replicated, may hold values from -0.25 to 0.25
Outputs:
- grid_out: bfloat16 [64, 2048, 512], P('band', 'patch')
The draws below stay inside these ranges and needn't reach their ends.
Inputs may be any that keep to these rules, and one draw needn't show every extreme that they name: `g2m_blocks`: the bands at both poles hold 16 live blocks in every sector. `g2m_sender`: never a latitude row before the first or after the last of the grid. `proc_sender`: below 2304, s % 256 is below 64 unless s // 256 = 4; never a band before the first or after the last. `dec_sender`: s % 256 is below 64 unless s // 256 = 4; never a band before the first or after the last.
All inputs are finite; a program needn't handle non-finite values.
Results may differ from the reference program's by a relative error of at most 0.0095.
Values may be sent and summed in bfloat16 or wider, within the bound.
No kernel may reach another device: no remote copies, remote signals or barrier semaphores. Data moves between devices by JAX's collectives and lax.ppermute only.
A program may use at most 128 MiB of HBM per device.

```python
import jax
import jax.numpy as jnp
from jax import lax

D = 512
LAT_DEV = 4
LON_DEV = 256
MESH_DEV = 256
COARSE_DEV = 16
G2M_DEV = 2048
PROC_DEV = 2048
HALO = 2
BORDER = 64
G2M_BLK = 16
BANDS = 16
PATCHES = 8
NLAT = 64
NLON = 2048
COARSE = 2048


def neighbour_slots(key, band_index, dims_shape, border_rows):
    pick_key, row_key = jax.random.split(key)
    pick_draw = jax.random.randint(pick_key, dims_shape, 0, 8, dtype=jnp.int32)
    neighbour = pick_draw + (pick_draw >= 4).astype(jnp.int32)
    neighbour = jnp.where((band_index == 0) & (neighbour < 3), neighbour + 6, neighbour)
    neighbour = jnp.where((band_index == BANDS - 1) & (neighbour >= 6), neighbour - 6, neighbour)
    row_draw = jax.random.randint(row_key, dims_shape, 0, border_rows, dtype=jnp.int32)
    return neighbour * MESH_DEV + row_draw


def draw_g2m_blocks(key, part):
    key = jax.random.fold_in(key, 11)
    band_index = jnp.arange(BANDS, dtype=jnp.int32)[:, None]
    distance = jnp.minimum(band_index, BANDS - 1 - band_index)
    jitter_top = max(2, G2M_BLK // 4 + 1)
    jitter = jax.random.randint(key, (BANDS, PATCHES), 0, jitter_top, dtype=jnp.int32) * (distance > 0).astype(jnp.int32)
    block_count = G2M_BLK - 3 * distance * G2M_BLK // BANDS - jitter
    return jnp.clip(block_count, max(1, G2M_BLK // 4), G2M_BLK).astype(jnp.int32)


def draw_g2m_sender(key, part):
    key = jax.random.fold_in(key, 12)
    row_key, col_key = jax.random.split(key)
    padded_width = LON_DEV + 2 * HALO
    dims_shape = (BANDS, PATCHES, G2M_DEV)
    band_index = jnp.arange(BANDS, dtype=jnp.int32)[:, None, None]
    low_row = jnp.where(band_index == 0, HALO, 0)
    high_row = jnp.where(band_index == BANDS - 1, LAT_DEV + HALO, LAT_DEV + 2 * HALO)
    row_draw = jax.random.randint(row_key, dims_shape, 0, 1 << 20, dtype=jnp.int32)
    row_draw = low_row + row_draw % (high_row - low_row)
    col_draw = jax.random.randint(col_key, dims_shape, 0, padded_width, dtype=jnp.int32)
    sender = row_draw * padded_width + col_draw
    sender = sender.at[1, 0, 0].set((LAT_DEV + 2 * HALO) * padded_width - 1)
    sender = sender.at[1, 0, 1].set(0)
    return sender.astype(jnp.int32)


def draw_g2m_receiver(key, part):
    key = jax.random.fold_in(key, 13)
    receiver = jax.random.randint(key, (BANDS, PATCHES, G2M_DEV), 0, MESH_DEV, dtype=jnp.int32)
    receiver = receiver.at[0, 0, 0].set(MESH_DEV - 1)
    receiver = receiver.at[0, 0, 1].set(0)
    return receiver


def draw_proc_sender(key, part):
    key = jax.random.fold_in(key, 14)
    kind_key, near_key, own_key, far_key = jax.random.split(key, 4)
    dims_shape = (BANDS, PATCHES, PROC_DEV)
    band_index = jnp.arange(BANDS, dtype=jnp.int32)[:, None, None]
    kind_draw = jax.random.randint(kind_key, dims_shape, 0, 8, dtype=jnp.int32)
    nearby = neighbour_slots(near_key, band_index, dims_shape, BORDER)
    own_rows = 4 * MESH_DEV + jax.random.randint(own_key, dims_shape, 0, MESH_DEV, dtype=jnp.int32)
    distant = 9 * MESH_DEV + jax.random.randint(far_key, dims_shape, 0, COARSE, dtype=jnp.int32)
    sender = jnp.where(kind_draw < 2, distant, jnp.where(kind_draw < 5, own_rows, nearby))
    sender = sender.at[1, 0, 0].set(9 * MESH_DEV + COARSE - 1)
    sender = sender.at[1, 0, 1].set(0)
    sender = sender.at[1, 0, 2].set(BORDER - 1)
    return sender.astype(jnp.int32)


def draw_proc_receiver(key, part):
    key = jax.random.fold_in(key, 15)
    receiver = jax.random.randint(key, (BANDS, PATCHES, PROC_DEV), 0, MESH_DEV, dtype=jnp.int32)
    receiver = receiver.at[0, 0, 0].set(MESH_DEV - 1)
    receiver = receiver.at[0, 0, 1].set(0)
    return receiver


def draw_dec_sender(key, part):
    key = jax.random.fold_in(key, 16)
    kind_key, near_key, own_key = jax.random.split(key, 3)
    dims_shape = (3, NLAT, NLON)
    band_index = (jnp.arange(NLAT, dtype=jnp.int32) // LAT_DEV)[None, :, None]
    kind_draw = jax.random.randint(kind_key, dims_shape, 0, 2, dtype=jnp.int32)
    nearby = neighbour_slots(near_key, band_index, dims_shape, BORDER)
    own_rows = 4 * MESH_DEV + jax.random.randint(own_key, dims_shape, 0, MESH_DEV, dtype=jnp.int32)
    sender = jnp.where(kind_draw == 0, own_rows, nearby)
    sender = sender.at[0, LAT_DEV, 0].set(8 * MESH_DEV + BORDER - 1)
    sender = sender.at[1, LAT_DEV, 0].set(0)
    return sender.astype(jnp.int32)


def levels(key, extent, cuts, smallest, top_value):
    loudness, own = 1.0, jax.random.fold_in(key, 6)
    for axis_at, blocks in cuts:
        draws = jnp.exp(jax.random.uniform(jax.random.fold_in(own, axis_at), (blocks,), jnp.float32, smallest / len(cuts), top_value / len(cuts)))
        loudness = loudness * jnp.repeat(draws, extent[axis_at] // blocks).reshape([-1 if axis == axis_at else 1 for axis in range(len(extent))])
    return loudness


def gaussian(key, shape, deviation, bound, cuts=(), kind=jnp.bfloat16):
    values = deviation * jax.random.normal(key, shape, jnp.float32)
    if cuts:
        values = values * levels(key, shape, cuts, -0.22, 0.18)
    return jnp.clip(values, -bound, bound).astype(kind)


def setup_inputs(seed: int = 0) -> dict:
    streams_of = jax.random.split(jax.random.key(seed), 15)
    return {
        "grid_state": gaussian(streams_of[0], (NLAT, NLON, D), 1.0, 6.0, ((0, 16), (1, 8))),
        "mesh_state": gaussian(streams_of[1], (BANDS, PATCHES, MESH_DEV, D), 1.0, 6.0, ((0, 16), (1, 8))),
        "g2m_features": gaussian(streams_of[2], (BANDS, PATCHES, G2M_DEV, D), 1.0, 6.0, ((0, 16), (1, 8))),
        "g2m_sender": draw_g2m_sender(jax.random.fold_in(streams_of[14], 71), 0),
        "g2m_receiver": draw_g2m_receiver(jax.random.fold_in(streams_of[14], 71), 0),
        "g2m_blocks": draw_g2m_blocks(jax.random.fold_in(streams_of[14], 71), 0),
        "proc_features": gaussian(streams_of[6], (BANDS, PATCHES, PROC_DEV, D), 1.0, 6.0, ((0, 16), (1, 8))),
        "proc_sender": draw_proc_sender(jax.random.fold_in(streams_of[14], 71), 0),
        "proc_receiver": draw_proc_receiver(jax.random.fold_in(streams_of[14], 71), 0),
        "dec_features": gaussian(streams_of[9], (3, NLAT, NLON, D), 1.0, 6.0, ((1, 16), (2, 8))),
        "dec_sender": draw_dec_sender(jax.random.fold_in(streams_of[14], 71), 0),
        "enc_weights": gaussian(streams_of[11], (9, D, D), D ** -0.5, 0.25),
        "proc_weights": gaussian(streams_of[12], (7, D, D), D ** -0.5, 0.25),
        "dec_weights": gaussian(streams_of[13], (7, D, D), D ** -0.5, 0.25),
    }


epsilon = 1e-05

def layer_norm(values):
    average = lax.optimization_barrier(jnp.mean(values, axis=-1, keepdims=True))
    centred = values - average
    spread = lax.optimization_barrier(jnp.mean(centred * centred, axis=-1, keepdims=True))
    return centred * lax.rsqrt(spread + epsilon)

def project(values, weight):
    matrix = values.reshape(-1, values.shape[-1])
    result = jnp.dot(matrix, weight, preferred_element_type=jnp.float32)
    return result.reshape(values.shape[:-1] + (weight.shape[1],))

def edge_message(features, send_rows, recv_rows, w_edge, w_out):
    before = project(features, w_edge) + send_rows.astype(jnp.float32) + recv_rows.astype(jnp.float32)
    hidden = jax.nn.silu(before).astype(jnp.bfloat16)
    return layer_norm(project(hidden, w_out)).astype(jnp.bfloat16)

def node_update(current, summed, w_self, w_total, w_out):
    before = project(current, w_self) + project(summed.astype(jnp.bfloat16), w_total)
    hidden = jax.nn.silu(before).astype(jnp.bfloat16)
    return (current.astype(jnp.float32) + layer_norm(project(hidden, w_out))).astype(jnp.bfloat16)

def self_update(current, w_first, w_out):
    hidden = jax.nn.silu(project(current, w_first)).astype(jnp.bfloat16)
    return (current.astype(jnp.float32) + layer_norm(project(hidden, w_out))).astype(jnp.bfloat16)

def close_rows(source, band_index, patch_index, sender):
    neighbour = sender // MESH_DEV
    src_band = (band_index + neighbour // 3 - 1) % BANDS
    src_patch = (patch_index + neighbour % 3 - 1) % PATCHES
    return source[src_band, src_patch, sender % MESH_DEV]

def reference(grid_state, mesh_state, g2m_features, g2m_sender, g2m_receiver, g2m_blocks, proc_features, proc_sender, proc_receiver, dec_features, dec_sender, enc_weights, proc_weights, dec_weights):
    padded_width = LON_DEV + 2 * HALO
    grid_send = project(grid_state, enc_weights[0]).astype(jnp.bfloat16)
    mesh_recv = project(mesh_state, enc_weights[1]).astype(jnp.bfloat16)
    wrapped = jnp.concatenate([grid_send[:, NLON - HALO:], grid_send, grid_send[:, :HALO]], axis=1)
    lat_rim = jnp.zeros((HALO, NLON + 2 * HALO, D), grid_send.dtype)
    padded = jnp.concatenate([lat_rim, wrapped, lat_rim], axis=0)
    devices = jnp.arange(BANDS * PATCHES, dtype=jnp.int32)

    def encode(device):
        band_index = device // PATCHES
        patch_index = device % PATCHES
        sender = g2m_sender[band_index, patch_index]
        receiver = g2m_receiver[band_index, patch_index]
        send_rows = padded[band_index * LAT_DEV + sender // padded_width, patch_index * LON_DEV + sender % padded_width]
        recv_rows = mesh_recv[band_index, patch_index][receiver]
        message = edge_message(g2m_features[band_index, patch_index], send_rows, recv_rows, enc_weights[2], enc_weights[3])
        live_mask = jnp.arange(G2M_DEV, dtype=jnp.int32) // 128 < g2m_blocks[band_index, patch_index]
        message = jnp.where(live_mask[:, None], message, jnp.zeros_like(message))
        return jax.ops.segment_sum(message.astype(jnp.float32), receiver, num_segments=MESH_DEV)
    enc_total = lax.map(encode, devices).reshape(BANDS, PATCHES, MESH_DEV, D)
    mesh_next = node_update(mesh_state, enc_total, enc_weights[4], enc_weights[5], enc_weights[6])
    grid_next = self_update(grid_state, enc_weights[7], enc_weights[8])
    proc_send = project(mesh_next, proc_weights[0]).astype(jnp.bfloat16)
    proc_recv = project(mesh_next, proc_weights[1]).astype(jnp.bfloat16)
    coarse = proc_send[:, :, MESH_DEV - COARSE_DEV:].reshape(COARSE, D)

    def process(device):
        band_index = device // PATCHES
        patch_index = device % PATCHES
        sender = proc_sender[band_index, patch_index]
        receiver = proc_receiver[band_index, patch_index]
        nearby = close_rows(proc_send, band_index, patch_index, jnp.minimum(sender, 9 * MESH_DEV - 1))
        distant = coarse[jnp.clip(sender - 9 * MESH_DEV, 0, COARSE - 1)]
        send_rows = jnp.where((sender < 9 * MESH_DEV)[:, None], nearby, distant)
        recv_rows = proc_recv[band_index, patch_index][receiver]
        message = edge_message(proc_features[band_index, patch_index], send_rows, recv_rows, proc_weights[2], proc_weights[3])
        return jax.ops.segment_sum(message.astype(jnp.float32), receiver, num_segments=MESH_DEV)
    proc_total = lax.map(process, devices).reshape(BANDS, PATCHES, MESH_DEV, D)
    mesh_last = node_update(mesh_next, proc_total, proc_weights[4], proc_weights[5], proc_weights[6])
    dec_send = project(mesh_last, dec_weights[0]).astype(jnp.bfloat16)
    dec_recv = project(grid_next, dec_weights[1]).astype(jnp.bfloat16)
    cell_band = (jnp.arange(NLAT, dtype=jnp.int32) // LAT_DEV)[:, None]
    cell_patch = (jnp.arange(NLON, dtype=jnp.int32) // LON_DEV)[None, :]
    dec_total = jnp.zeros((NLAT, NLON, D), jnp.float32)
    for which in range(3):
        send_rows = close_rows(dec_send, cell_band, cell_patch, dec_sender[which])
        message = edge_message(dec_features[which], send_rows, dec_recv, dec_weights[2], dec_weights[3])
        dec_total = dec_total + message.astype(jnp.float32)
    return node_update(grid_next, dec_total, dec_weights[4], dec_weights[5], dec_weights[6])
```

```python
import jax
import jax.numpy as jnp
from jax import lax
from jax.experimental import pallas as pl
from jax.experimental.pallas import tpu as pltpu
from jax.sharding import PartitionSpec as P

D = 512
AXES = ("band", "patch")
BANDS, PATCHES = 16, 8
EDGE_BLOCK = 256
epsilon = 1e-05
F32, BF16 = jnp.float32, jnp.bfloat16


def split(device):
    band, patch = divmod(device, PATCHES)
    return band // 4, band % 4, patch // 2, patch % 2


def torus(dy=0, dz=0, dx=0, dc=0):
    pairs = []
    for device in range(BANDS * PATCHES):
        y, z, x, c = split(device)
        band = (y + dy) % 4 * 4 + (z + dz) % 4
        patch = (x + dx) % 4 * 2 + (c + dc) % 2
        pairs.append((device, band * PATCHES + patch))
    return pairs


def plane(db, dp):
    return [
        (b * PATCHES + p, (b + db) % BANDS * PATCHES + (p + dp) % PATCHES)
        for b in range(BANDS)
        for p in range(PATCHES)
    ]


def send(values, pairs):
    return lax.ppermute(values, AXES, pairs)


def dot(a, b):
    return jnp.dot(a, b, preferred_element_type=F32)


def silu(v):
    half = 0.5 * v
    return half + half * jnp.tanh(half)


def layer_norm(v):
    centred = v - jnp.mean(v, axis=-1, keepdims=True)
    spread = jnp.mean(centred * centred, axis=-1, keepdims=True)
    return centred * lax.rsqrt(spread + epsilon)


def column(row):
    return jnp.transpose(jnp.broadcast_to(row, (8, row.shape[1])))[:, :1]


def pick_rows(row, count):
    col = column(row)
    lanes = lax.broadcasted_iota(jnp.int32, (row.shape[1], count), 1)
    return jnp.where(lanes == col, 1.0, 0.0).astype(BF16)


def add_rows(row, count):
    nodes = lax.broadcasted_iota(jnp.int32, (count, row.shape[1]), 0)
    return jnp.where(nodes == row, 1.0, 0.0).astype(BF16)


def weight(k):
    return pl.BlockSpec((None, D, D), lambda i: (k, 0, 0))


def whole(shape):
    return pl.BlockSpec(shape, lambda i: (0,) * len(shape))


def params(mb):
    return pltpu.CompilerParams(
        dimension_semantics=("arbitrary",), vmem_limit_bytes=mb << 20
    )


def cost(rows, nbytes):
    return pl.CostEstimate(flops=2 * rows * D * D, bytes_accessed=nbytes, transcendentals=0)


def grid_body(x_ref, w0, w7, w8, d1, sent, nxt, recv):
    x = x_ref[...]
    sent[...] = dot(x, w0[...]).astype(BF16)
    hidden = silu(dot(x, w7[...])).astype(BF16)
    y = (x.astype(F32) + layer_norm(dot(hidden, w8[...]))).astype(BF16)
    nxt[...] = y
    recv[...] = dot(y, d1[...]).astype(BF16)


def grid_kernel(grid_flat, enc_w, dec_w):
    blk = pl.BlockSpec((256, D), lambda i: (i, 0))
    return pl.pallas_call(
        grid_body,
        grid=(4,),
        in_specs=[blk, weight(0), weight(7), weight(8), weight(1)],
        out_specs=[blk] * 3,
        out_shape=[jax.ShapeDtypeStruct((1024, D), BF16)] * 3,
        compiler_params=params(24),
        cost_estimate=cost(4096, 6 << 20),
        name="grid_cells",
    )(grid_flat, enc_w, enc_w, enc_w, dec_w)


def enc_body(
    live, feat, snd, rcv, own, top, bottom, side, mesh_ref,
    w0, w1, w2, w3, w4, w5, w6, p0, p1,
    nxt, psend, precv, table, total,
):
    step = pl.program_id(0)

    @pl.when(step == 0)
    def _():
        table[0:512] = dot(top[...], w0[...]).astype(BF16)
        table[512:1536] = own[...]
        table[1536:2048] = dot(bottom[...], w0[...]).astype(BF16)
        table[2048:2080] = dot(side[...], w0[...]).astype(BF16)
        table[2080:2176] = jnp.zeros((96, D), BF16)
        table[2176:2432] = dot(mesh_ref[...], w1[...]).astype(BF16)
        total[...] = jnp.zeros_like(total)

    receiver = rcv[...]
    ones = jnp.concatenate([pick_rows(snd[...], 2176), pick_rows(receiver, 256)], axis=1)
    before = dot(feat[...], w2[...]) + dot(ones, table[...])
    hidden = silu(before).astype(BF16)
    message = layer_norm(dot(hidden, w3[...])).astype(BF16)
    edge = step * EDGE_BLOCK + lax.broadcasted_iota(jnp.int32, (1, EDGE_BLOCK), 1)
    target = jnp.where(edge < live[0] * 128, receiver, -1)
    total[...] += dot(add_rows(target, 256), message)

    @pl.when(step == pl.num_programs(0) - 1)
    def _():
        m = mesh_ref[...]
        hid = silu(dot(m, w4[...]) + dot(total[...].astype(BF16), w5[...])).astype(BF16)
        new = (m.astype(F32) + layer_norm(dot(hid, w6[...]))).astype(BF16)
        nxt[...] = new
        psend[...] = dot(new, p0[...]).astype(BF16)
        precv[...] = dot(new, p1[...]).astype(BF16)


def edge_rows():
    return pl.BlockSpec((None, 1, EDGE_BLOCK), lambda i: (i, 0, 0))


def enc_kernel(live, feats, senders, receivers, own, top, bottom, side, mesh_flat, enc_w, proc_w):
    steps = feats.shape[0] // EDGE_BLOCK
    node = whole((256, D))
    return pl.pallas_call(
        enc_body,
        grid=(steps,),
        in_specs=[
            pl.BlockSpec(memory_space=pltpu.SMEM),
            pl.BlockSpec((EDGE_BLOCK, D), lambda i: (i, 0)),
            edge_rows(),
            edge_rows(),
            whole((1024, D)),
            whole((512, D)),
            whole((512, D)),
            whole((32, D)),
            node,
        ]
        + [weight(k) for k in range(7)]
        + [weight(0), weight(1)],
        out_specs=[node] * 3,
        out_shape=[jax.ShapeDtypeStruct((256, D), BF16)] * 3,
        scratch_shapes=[pltpu.VMEM((2432, D), BF16), pltpu.VMEM((256, D), F32)],
        compiler_params=params(40),
        cost_estimate=cost(16000, 10 << 20),
        name="encoder_edges",
    )(
        live, feats, senders.reshape(steps, 1, -1), receivers.reshape(steps, 1, -1),
        own, top, bottom, side, mesh_flat, *[enc_w] * 7, proc_w, proc_w,
    )


def proc_body(
    feat, snd, rcv, mine, theirs, near, recv, mesh_ref,
    w2, w3, w4, w5, w6, d0,
    dsend, table, total,
):
    step = pl.program_id(0)

    @pl.when(step == 0)
    def _():
        table[0:1024] = mine[...]
        table[1024:2048] = theirs[...]
        table[2048:2816] = near[...]
        table[2816:3072] = recv[...]
        total[...] = jnp.zeros_like(total)

    receiver = rcv[...]
    ones = jnp.concatenate([pick_rows(snd[...], 2816), pick_rows(receiver, 256)], axis=1)
    before = dot(feat[...], w2[...]) + dot(ones, table[...])
    hidden = silu(before).astype(BF16)
    message = layer_norm(dot(hidden, w3[...])).astype(BF16)
    total[...] += dot(add_rows(receiver, 256), message)

    @pl.when(step == pl.num_programs(0) - 1)
    def _():
        m = mesh_ref[...]
        hid = silu(dot(m, w4[...]) + dot(total[...].astype(BF16), w5[...])).astype(BF16)
        new = (m.astype(F32) + layer_norm(dot(hid, w6[...]))).astype(BF16)
        dsend[...] = dot(new, d0[...]).astype(BF16)


def proc_kernel(feats, senders, receivers, mine, theirs, near, recv, mesh_next, proc_w, dec_w):
    steps = feats.shape[0] // EDGE_BLOCK
    node = whole((256, D))

    return pl.pallas_call(
        proc_body,
        grid=(steps,),
        in_specs=[
            pl.BlockSpec((EDGE_BLOCK, D), lambda i: (i, 0)),
            edge_rows(),
            edge_rows(),
            whole((1024, D)),
            whole((1024, D)),
            whole((768, D)),
            node,
            node,
        ]
        + [weight(k) for k in range(2, 7)]
        + [weight(0)],
        out_specs=node,
        out_shape=jax.ShapeDtypeStruct((256, D), BF16),
        scratch_shapes=[pltpu.VMEM((3072, D), BF16), pltpu.VMEM((256, D), F32)],
        compiler_params=params(40),
        cost_estimate=cost(19000, 10 << 20),
        name="mesh_edges",
    )(
        feats, senders.reshape(steps, 1, -1), receivers.reshape(steps, 1, -1),
        mine, theirs, near, recv, mesh_next, *[proc_w] * 5, dec_w,
    )


def dec_body(feat, snd, near, recv, cells, w2, w3, w4, w5, w6, out):
    r = recv[...].astype(F32)
    summed = None
    for k in range(3):
        before = dot(feat[k], w2[...]) + dot(pick_rows(snd[k], 768), near[...]) + r
        hidden = silu(before).astype(BF16)
        message = layer_norm(dot(hidden, w3[...])).astype(BF16).astype(F32)
        summed = message if summed is None else summed + message
    g = cells[...]
    hid = silu(dot(g, w4[...]) + dot(summed.astype(BF16), w5[...])).astype(BF16)
    out[...] = (g.astype(F32) + layer_norm(dot(hid, w6[...]))).astype(BF16)


def dec_kernel(feats, senders, near, recv, grid_next, dec_w):
    lat, lon = senders.shape[1:]
    blk = pl.BlockSpec((lon, D), lambda i: (i, 0))
    return pl.pallas_call(
        dec_body,
        grid=(lat,),
        in_specs=[
            pl.BlockSpec((3, None, lon, D), lambda i: (0, i, 0, 0)),
            pl.BlockSpec((3, None, 1, lon), lambda i: (0, i, 0, 0)),
            whole((768, D)),
            blk,
            blk,
        ]
        + [weight(k) for k in range(2, 7)],
        out_specs=blk,
        out_shape=jax.ShapeDtypeStruct((lat * lon, D), BF16),
        compiler_params=params(40),
        cost_estimate=cost(15000, 9 << 20),
        name="decoder_edges",
    )(feats, senders.reshape(3, lat, 1, lon), near, recv, grid_next, *[dec_w] * 5)


def near_rows(own):
    rim = own[:64]
    above, below = send(rim, plane(1, 0)), send(rim, plane(-1, 0))
    col = jnp.concatenate([above, rim, below], axis=0)
    left, right = send(col, plane(0, 1)), send(col, plane(0, -1))
    return jnp.concatenate([above, own, below, left, right], axis=0)


def near_index(sender):
    q, r = sender // 256, sender % 256
    row, col = q // 3, q % 3
    middle = jnp.where(row == 0, 0, jnp.where(row == 1, 64, 320))
    aside = jnp.where(col == 0, 384, 576) + row * 64
    return jnp.where(col == 1, middle, aside) + r


def coarse_rows(rows):
    for axis in ("dx", "dy"):
        rows = jnp.concatenate(
            [rows] + [send(rows, torus(**{axis: k})) for k in (1, 2, 3)], axis=0
        )
    mine = jnp.concatenate([rows] + [send(rows, torus(dz=k)) for k in (1, 2, 3)], axis=0)
    return mine, send(mine, torus(dc=1))


def coarse_index(c):
    band, patch = lax.axis_index("band"), lax.axis_index("patch")
    device, row = c // 16, c % 16
    b, p = device // PATCHES, device % PATCHES
    ky = (band // 4 - b // 4) % 4
    kz = (band % 4 - b % 4) % 4
    kx = (patch // 2 - p // 2) % 4
    kc = (patch % 2 - p % 2) % 2
    return kc * 1024 + kz * 256 + ky * 64 + kx * 16 + row


def shards(
    grid_state,
    mesh_state,
    g2m_features,
    g2m_sender,
    g2m_receiver,
    g2m_blocks,
    proc_features,
    proc_sender,
    proc_receiver,
    dec_features,
    dec_sender,
    enc_weights,
    proc_weights,
    dec_weights,
):
    cells = grid_state.reshape(1024, D)
    nodes = mesh_state.reshape(256, D)
    top = send(grid_state[2:4], plane(1, 0))
    bottom = send(grid_state[0:2], plane(-1, 0))
    west = send(grid_state[:, 254:256], plane(0, 1))
    east = send(grid_state[:, 0:2], plane(0, -1))
    flank = jnp.concatenate([west, east], axis=1)
    side = jnp.concatenate(
        [send(flank[2:4], plane(1, 0)), flank, send(flank[0:2], plane(-1, 0))], axis=0
    ).reshape(32, D)
    s = g2m_sender.reshape(-1)
    i, j = s // 260, s % 260
    inner = (j >= 2) & (j < 258)
    enc_sender = jnp.where(
        inner, i * 256 + j - 2, 2048 + i * 4 + jnp.where(j < 2, j, j - 256)
    )
    s = proc_sender.reshape(-1)
    mesh_sender = jnp.where(
        s < 2304, 2048 + near_index(jnp.minimum(s, 2303)), coarse_index(jnp.maximum(s - 2304, 0))
    )
    grid_sender = near_index(dec_sender)
    live = g2m_blocks[lax.axis_index("band"), lax.axis_index("patch")].reshape(1)

    grid_send, grid_next, dec_recv = grid_kernel(cells, enc_weights, dec_weights)
    mesh_next, proc_send, proc_recv = enc_kernel(
        live, g2m_features.reshape(-1, D), enc_sender, g2m_receiver.reshape(-1),
        grid_send, top.reshape(512, D), bottom.reshape(512, D), side, nodes,
        enc_weights, proc_weights,
    )
    mine, theirs = coarse_rows(proc_send[240:256])
    dec_send = proc_kernel(
        proc_features.reshape(-1, D), mesh_sender, proc_receiver.reshape(-1),
        mine, theirs, near_rows(proc_send), proc_recv, mesh_next, proc_weights, dec_weights,
    )
    out = dec_kernel(
        dec_features, grid_sender, near_rows(dec_send), dec_recv, grid_next, dec_weights
    )
    return out.reshape(grid_state.shape)


def solution(mesh):
    placed = (
        P("band", "patch", None),
        P("band", "patch", None, None),
        P("band", "patch", None, None),
        P("band", "patch", None),
        P("band", "patch", None),
        P(),
        P("band", "patch", None, None),
        P("band", "patch", None),
        P("band", "patch", None),
        P(None, "band", "patch", None),
        P(None, "band", "patch"),
        P(),
        P(),
        P(),
    )
    return jax.shard_map(
        shards, mesh=mesh, in_specs=placed, out_specs=P("band", "patch", None), check_vma=False
    )
```

```python
import jax
import jax.numpy as jnp
from jax import lax
from jax.experimental import pallas as pl
from jax.experimental.pallas import tpu as pltpu
from jax.sharding import PartitionSpec as P

D = 512
AXES = ("band", "patch")
BANDS, PATCHES = 16, 8
EDGE_BLOCK = 1024
epsilon = 1e-05
F32, BF16 = jnp.float32, jnp.bfloat16


def split(device):
    band, patch = device // PATCHES, device % PATCHES
    return band // 4, band % 4, patch // 2, patch % 2


def torus(dy=0, dz=0, dx=0, dc=0):
    pairs = []
    for device in range(BANDS * PATCHES):
        y, z, x, c = split(device)
        band = (y + dy) % 4 * 4 + (z + dz) % 4
        patch = (x + dx) % 4 * 2 + (c + dc) % 2
        pairs.append((device, band * PATCHES + patch))
    return pairs


def plane(db, dp):
    return [
        (b * PATCHES + p, (b + db) % BANDS * PATCHES + (p + dp) % PATCHES)
        for b in range(BANDS)
        for p in range(PATCHES)
    ]


def send(values, pairs):
    return lax.ppermute(values, AXES, pairs)


def dot(a, b):
    return jnp.dot(a, b, preferred_element_type=F32)


def silu(v):
    half = 0.5 * v
    return half + half * jnp.tanh(half)


def layer_norm(v):
    centred = v - jnp.mean(v, axis=-1, keepdims=True)
    spread = jnp.mean(centred * centred, axis=-1, keepdims=True)
    return centred * lax.rsqrt(spread + epsilon)


def column(row):
    return jnp.transpose(jnp.broadcast_to(row, (8, row.shape[1])))[:, :1]


def pick_rows(row, count):
    col = column(row)
    lanes = lax.broadcasted_iota(jnp.int32, (row.shape[1], count), 1)
    return jnp.where(lanes == col, 1.0, 0.0).astype(BF16)


def add_rows(row, count):
    nodes = lax.broadcasted_iota(jnp.int32, (count, row.shape[1]), 0)
    return jnp.where(nodes == row, 1.0, 0.0).astype(BF16)


def weight(k):
    return pl.BlockSpec((None, D, D), lambda i: (k, 0, 0))


class Fetched:
    def __init__(self, source, target, sem):
        self.copy, self.target, self.ready = pltpu.make_async_copy(source, target, sem), target, False
        self.copy.start()

    def __call__(self):
        if not self.ready:
            self.copy.wait()
            self.ready = True
        return self.target


def whole(shape):
    return pl.BlockSpec(shape, lambda i: (0,) * len(shape))


def params(mb):
    return pltpu.CompilerParams(
        dimension_semantics=("arbitrary",), vmem_limit_bytes=mb << 20
    )


def cost(rows, nbytes):
    return pl.CostEstimate(flops=2 * rows * D * D, bytes_accessed=nbytes, transcendentals=0)


def grid_body(x_ref, w0, w7, w8, sent, nxt):
    x = x_ref[...]
    sent[...] = dot(x, w0[...]).astype(BF16)
    hidden = silu(dot(x, w7[...])).astype(BF16)
    nxt[...] = (x.astype(F32) + layer_norm(dot(hidden, w8[...]))).astype(BF16)


def grid_kernel(grid_flat, enc_w):
    blk = pl.BlockSpec((512, D), lambda i: (i, 0))
    return pl.pallas_call(
        grid_body,
        grid=(2,),
        in_specs=[blk, weight(0), weight(7), weight(8)],
        out_specs=[blk] * 2,
        out_shape=[jax.ShapeDtypeStruct((1024, D), BF16)] * 2,
        compiler_params=params(60),
        cost_estimate=cost(5000, 5 << 20),
        name="grid_cells",
    )(grid_flat, *[enc_w] * 3)


def lead_body(feat, cells, d1, w2, w4, before, self_part):
    g = cells[...]
    recv = dot(g, d1[...]).astype(BF16).astype(F32)
    self_part[...] = dot(g, w4[...])
    for k in range(3):
        before[k] = (dot(feat[k], w2[...]) + recv).astype(before.dtype)


def lead_kernel(feats, grid_next, dec_w):
    lat, lon = feats.shape[1:3]
    blk = pl.BlockSpec((lon, D), lambda i: (i, 0))
    edges = pl.BlockSpec((3, None, lon, D), lambda i: (0, i, 0, 0))
    return pl.pallas_call(
        lead_body,
        grid=(lat,),
        in_specs=[edges, blk, weight(1), weight(2), weight(4)],
        out_specs=[edges, blk],
        out_shape=[
            jax.ShapeDtypeStruct(feats.shape, BF16),
            jax.ShapeDtypeStruct(grid_next.shape, F32),
        ],
        compiler_params=params(60),
        cost_estimate=cost(8000, 10 << 20),
        name="decoder_lead",
    )(feats, grid_next, *[dec_w] * 3)


def edge_sum(before, hidden_weight, target):
    hidden = silu(before).astype(BF16)
    message = layer_norm(dot(hidden, hidden_weight)).astype(BF16)
    return dot(add_rows(target, 256), message)


def node_update(m, total, w4, w5, w6):
    hid = silu(dot(m, w4()[...]) + dot(total.astype(BF16), w5()[...])).astype(BF16)
    return (m.astype(F32) + layer_norm(dot(hid, w6()[...]))).astype(BF16)


def enc_body(
    live, snd, rcv, feat, own, top, bottom, side, mesh_ref, enc_w, proc_w,
    nxt, psend, precv,
    table, feat_v, rim_v, side_v, mesh_v, weights, sems,
):
    count = iter(range(sems.shape[0]))

    def fetch(source, target):
        return Fetched(source, target, sems.at[next(count)])

    steps = feat.shape[0] // EDGE_BLOCK
    w0 = fetch(enc_w.at[0], weights.at[0])
    rims = [fetch(top, rim_v.at[0]), fetch(bottom, rim_v.at[1])]
    sides = fetch(side, side_v)
    mesh = fetch(mesh_ref, mesh_v)
    w1 = fetch(enc_w.at[1], weights.at[1])
    mine = fetch(own, table.at[pl.ds(512, 1024)])
    w2, w3 = (fetch(enc_w.at[k], weights.at[k]) for k in (2, 3))
    feats = []
    for k in range(steps):
        rows = pl.ds(k * EDGE_BLOCK, EDGE_BLOCK)
        feats.append(fetch(feat.at[rows], feat_v.at[rows]))
    w4, w5, w6 = (fetch(enc_w.at[k], weights.at[k]) for k in (4, 5, 6))
    p0, p1 = (fetch(proc_w.at[k], weights.at[7 + k]) for k in (0, 1))

    table[2080:2176] = jnp.zeros((96, D), BF16)
    table[0:512] = dot(rims[0]()[...], w0()[...]).astype(BF16)
    table[1536:2048] = dot(rims[1]()[...], w0()[...]).astype(BF16)
    table[2048:2080] = dot(sides()[...], w0()[...]).astype(BF16)
    table[2176:2432] = dot(mesh()[...], w1()[...]).astype(BF16)
    mine()
    for ready in (w2, w3, *feats):
        ready()
    alive = live[lax.axis_index("band"), lax.axis_index("patch")] * 128

    def edges(k, total):
        receiver = rcv[k]
        ones = jnp.concatenate([pick_rows(snd[k], 2176), pick_rows(receiver, 256)], axis=1)
        x = feat_v[pl.ds(pl.multiple_of(k * EDGE_BLOCK, EDGE_BLOCK), EDGE_BLOCK)]
        before = dot(x, w2()[...]) + dot(ones, table[...])
        edge = k * EDGE_BLOCK + lax.broadcasted_iota(jnp.int32, (1, EDGE_BLOCK), 1)
        return total + edge_sum(before, w3()[...], jnp.where(edge < alive, receiver, -1))

    total = lax.fori_loop(0, steps, edges, jnp.zeros((256, D), F32))
    new = node_update(mesh()[...], total, w4, w5, w6)
    psend[...] = dot(new, p0()[...]).astype(BF16)
    nxt[...] = new
    precv[...] = dot(new, p1()[...]).astype(BF16)


SMEM = pl.BlockSpec(memory_space=pltpu.SMEM)
VMEM = pl.BlockSpec(memory_space=pltpu.VMEM)
HBM = pl.BlockSpec(memory_space=pl.ANY)


def edge_rows(index):
    return index.reshape(-1, 1, EDGE_BLOCK)


def enc_kernel(live, feats, senders, receivers, own, top, bottom, side, mesh_flat, enc_w, proc_w):
    return pl.pallas_call(
        enc_body,
        in_specs=[SMEM, VMEM, VMEM] + [HBM] * 8,
        out_specs=[VMEM] * 3,
        out_shape=[jax.ShapeDtypeStruct((256, D), BF16)] * 3,
        scratch_shapes=[
            pltpu.VMEM((2432, D), BF16),
            pltpu.VMEM(feats.shape, BF16),
            pltpu.VMEM((2, 512, D), BF16),
            pltpu.VMEM((32, D), BF16),
            pltpu.VMEM((256, D), BF16),
            pltpu.VMEM((9, D, D), BF16),
            pltpu.SemaphoreType.DMA((15 + feats.shape[0] // EDGE_BLOCK,)),
        ],
        compiler_params=pltpu.CompilerParams(vmem_limit_bytes=60 << 20),
        cost_estimate=cost(25000, 10 << 20),
        name="encoder_edges",
    )(
        live, edge_rows(senders), edge_rows(receivers),
        feats, own, top, bottom, side, mesh_flat, enc_w, proc_w,
    )


COARSE = ((0, 256), (256, 256), (512, 256), (768, 128), (896, 128))
NEAR = ((2048, 64), (2112, 256), (2368, 64), (2432, 192), (2624, 192))


def proc_body(*refs):
    snd, rcv, feat = refs[:3]
    pieces, (recv, mesh_ref, proc_w, dec_w) = refs[3:18], refs[18:22]
    dsend, table, feat_v, mesh_v, weights, sems = refs[22:]
    count = iter(range(sems.shape[0]))

    def fetch(source, target):
        return Fetched(source, target, sems.at[next(count)])

    places = COARSE + tuple((at + 1024, rows) for at, rows in COARSE) + NEAR
    first = [fetch(recv, table.at[pl.ds(2816, 256)])]
    for piece, (at, rows) in zip(pieces, places):
        first.append(fetch(piece.at[pl.ds(0, rows)], table.at[pl.ds(at, rows)]))
    first += [fetch(proc_w.at[k], weights.at[k - 2]) for k in (2, 3)]
    first.append(fetch(feat, feat_v))
    mesh = fetch(mesh_ref, mesh_v)
    w4, w5, w6 = (fetch(proc_w.at[k], weights.at[k - 2]) for k in (4, 5, 6))
    d0 = fetch(dec_w.at[0], weights.at[5])
    for ready in first:
        ready()

    def edges(k, total):
        receiver = rcv[k]
        ones = jnp.concatenate([pick_rows(snd[k], 2816), pick_rows(receiver, 256)], axis=1)
        x = feat_v[pl.ds(pl.multiple_of(k * EDGE_BLOCK, EDGE_BLOCK), EDGE_BLOCK)]
        before = dot(x, weights[0]) + dot(ones, table[...])
        return total + edge_sum(before, weights[1], receiver)

    total = lax.fori_loop(0, snd.shape[0], edges, jnp.zeros((256, D), F32))
    new = node_update(mesh()[...], total, w4, w5, w6)
    dsend[...] = dot(new, d0()[...]).astype(BF16)


def proc_kernel(feats, senders, receivers, pieces, recv, mesh_next, proc_w, dec_w):
    return pl.pallas_call(
        proc_body,
        in_specs=[VMEM, VMEM] + [HBM] * 20,
        out_specs=VMEM,
        out_shape=jax.ShapeDtypeStruct((256, D), BF16),
        scratch_shapes=[
            pltpu.VMEM((3072, D), BF16),
            pltpu.VMEM(feats.shape, BF16),
            pltpu.VMEM((256, D), BF16),
            pltpu.VMEM((6, D, D), BF16),
            pltpu.SemaphoreType.DMA((24,)),
        ],
        compiler_params=pltpu.CompilerParams(vmem_limit_bytes=60 << 20),
        cost_estimate=cost(25000, 10 << 20),
        name="mesh_edges",
    )(
        edge_rows(senders), edge_rows(receivers), feats, *pieces, recv, mesh_next, proc_w, dec_w,
    )


def dec_body(snd, lead, above, own, below, beside, across, cells, self_part, w3, w5, w6, out, near):
    @pl.when(pl.program_id(0) == 0)
    def _():
        near[0:64] = above[...]
        near[64:320] = own[...]
        near[320:384] = below[...]
        near[384:576] = beside[...]
        near[576:768] = across[...]

    n = cells.shape[0]
    ones = jnp.concatenate([pick_rows(snd[k], 768) for k in range(3)], axis=0)
    before = lead[...].astype(F32).reshape(3 * n, D) + dot(ones, near[...])
    hidden = silu(before).astype(BF16)
    message = layer_norm(dot(hidden, w3[...])).astype(BF16).astype(F32).reshape(3, n, D)
    summed = message[0] + message[1] + message[2]
    hid = silu(self_part[...] + dot(summed.astype(BF16), w5[...])).astype(BF16)
    out[...] = (cells[...].astype(F32) + layer_norm(dot(hid, w6[...]))).astype(BF16)


def dec_kernel(lead, senders, near, grid_next, self_part, dec_w):
    lat, lon = senders.shape[1:]
    blk = pl.BlockSpec((lon, D), lambda i: (i, 0))
    return pl.pallas_call(
        dec_body,
        grid=(lat,),
        in_specs=[
            pl.BlockSpec((3, None, 1, lon), lambda i: (0, i, 0, 0)),
            pl.BlockSpec((3, None, lon, D), lambda i: (0, i, 0, 0)),
        ]
        + [whole(rows.shape) for rows in near]
        + [blk, blk, weight(3), weight(5), weight(6)],
        out_specs=blk,
        out_shape=jax.ShapeDtypeStruct((lat * lon, D), BF16),
        scratch_shapes=[pltpu.VMEM((768, D), BF16)],
        compiler_params=params(60),
        cost_estimate=cost(15000, 9 << 20),
        name="decoder_edges",
    )(senders.reshape(3, lat, 1, lon), lead, *near, grid_next, self_part, *[dec_w] * 3)


SWAP = [(d, d ^ 1) for d in range(BANDS * PATCHES)]
CROSS = [
    (d, d // PATCHES * PATCHES + (d % PATCHES + (1 if d % 2 else -1)) % PATCHES)
    for d in range(BANDS * PATCHES)
]


def on_chip(col):
    return (col == 2) == (lax.axis_index("patch") % 2 == 0)


def near_index(sender):
    q, r = sender // 256, sender % 256
    row, col = q // 3, q % 3
    middle = jnp.where(row == 0, 0, jnp.where(row == 1, 64, 320))
    return jnp.where(col == 1, middle, jnp.where(on_chip(col), 384, 576) + row * 64) + r


def mesh_index(sender):
    device, node = jnp.maximum(sender - 2304, 0) // 16, sender % 16
    y, z, x, c = split(device)
    my_y, my_z, my_x, my_c = split(lax.axis_index("band") * PATCHES + lax.axis_index("patch"))
    kx, kz, kc = (my_x - x) % 4, (my_z - z) % 4, (my_c - c) % 2
    turn = jnp.where((kz == 1) & (my_z == 0), -1, 0) + jnp.where((kz == 3) & (my_z == 3), 1, 0)
    ky = (my_y - y + turn) % 4
    ky, kz = (jnp.where(k < 2, k, 5 - k) for k in (ky, kz))
    far = kc * 1024 + ky * 256 + kx * 64 + kz * 16 + node
    return jnp.where(sender < 2304, 2048 + near_index(jnp.minimum(sender, 2303)), far)


def mesh_rows(own, lead):
    rim, rows = own[:64], own[240:256]
    both = jnp.concatenate([rim, rows], axis=0)
    above, below = send(both, plane(1, 0)), send(both, plane(-1, 0))
    rows = jnp.concatenate([rows, above[64:], below[64:], send(rows, torus(dz=2))], axis=0)
    here = jnp.concatenate([rows] + [send(rows, torus(dx=k)) for k in (1, 2, 3)], axis=0)
    col = jnp.concatenate([above[:64], rim, below[:64]], axis=0)
    beside, across = send(col, SWAP), send(col, CROSS)
    here, given = lax.optimization_barrier((here, lead[0]))
    lead = lead[1](given)
    ahead, behind = send(here, torus(dy=1)), send(here, torus(dy=-1))
    ahead, behind, lead = lax.optimization_barrier((ahead, behind, lead))
    far = send(ahead[:128], torus(dy=1)), send(behind[128:], torus(dy=-1))
    coarse = [here, ahead, behind, *far]
    return coarse + [send(v, SWAP) for v in coarse] + [above, own, below, beside, across], lead


def near_rows(own):
    rim = own[:64]
    above, below = send(rim, plane(1, 0)), send(rim, plane(-1, 0))
    col = jnp.concatenate([above, rim, below], axis=0)
    return above, own, below, send(col, SWAP), send(col, CROSS)


def shards(
    grid_state,
    mesh_state,
    g2m_features,
    g2m_sender,
    g2m_receiver,
    g2m_blocks,
    proc_features,
    proc_sender,
    proc_receiver,
    dec_features,
    dec_sender,
    enc_weights,
    proc_weights,
    dec_weights,
):
    cells = grid_state.reshape(1024, D)
    nodes = mesh_state.reshape(256, D)
    top = send(grid_state[2:4], plane(1, 0))
    bottom = send(grid_state[0:2], plane(-1, 0))
    first = jnp.concatenate([top[:, :2], grid_state[:, :2], bottom[:, :2]], axis=0)
    final = jnp.concatenate([top[:, 254:], grid_state[:, 254:], bottom[:, 254:]], axis=0)
    west, east = send(final, plane(0, 1)), send(first, plane(0, -1))
    side = jnp.concatenate([west, east], axis=1).reshape(32, D)
    s = g2m_sender.reshape(-1)
    i, j = s // 260, s % 260
    inner = (j >= 2) & (j < 258)
    enc_sender = jnp.where(
        inner, i * 256 + j - 2, 2048 + i * 4 + jnp.where(j < 2, j, j - 256)
    )
    proc_sender, proc_receiver = proc_sender.reshape(-1), proc_receiver.reshape(-1)

    grid_send, grid_next = grid_kernel(cells, enc_weights)
    mesh_next, proc_send, proc_recv = enc_kernel(
        g2m_blocks, g2m_features.reshape(-1, D), enc_sender, g2m_receiver.reshape(-1),
        grid_send, top.reshape(512, D), bottom.reshape(512, D), side, nodes,
        enc_weights, proc_weights,
    )
    pieces, (lead, self_part) = mesh_rows(
        proc_send, (grid_next, lambda g: lead_kernel(dec_features, g, dec_weights))
    )
    dec_send = proc_kernel(
        proc_features.reshape(-1, D), mesh_index(proc_sender), proc_receiver, pieces, proc_recv,
        mesh_next, proc_weights, dec_weights,
    )
    out = dec_kernel(
        lead, near_index(dec_sender), near_rows(dec_send), grid_next, self_part, dec_weights
    )
    return out.reshape(grid_state.shape)


def solution(mesh):
    placed = (
        P("band", "patch", None),
        P("band", "patch", None, None),
        P("band", "patch", None, None),
        P("band", "patch", None),
        P("band", "patch", None),
        P(),
        P("band", "patch", None, None),
        P("band", "patch", None),
        P("band", "patch", None),
        P(None, "band", "patch", None),
        P(None, "band", "patch"),
        P(),
        P(),
        P(),
    )
    return jax.shard_map(
        shards, mesh=mesh, in_specs=placed, out_specs=P("band", "patch", None), check_vma=False
    )
```

```python
import jax
import jax.numpy as jnp
from jax import lax
from jax.experimental import pallas as pl
from jax.experimental.pallas import tpu as pltpu
from jax.sharding import PartitionSpec as P

D = 512
AXES = ("band", "patch")
BANDS, PATCHES = 16, 8
EDGE_BLOCK = 1024
epsilon = 1e-05
F32, BF16 = jnp.float32, jnp.bfloat16


def split(device):
    band, patch = device // PATCHES, device % PATCHES
    return band // 4, band % 4, patch // 2, patch % 2


def torus(dy=0, dz=0, dx=0, dc=0):
    pairs = []
    for device in range(BANDS * PATCHES):
        y, z, x, c = split(device)
        band = (y + dy) % 4 * 4 + (z + dz) % 4
        patch = (x + dx) % 4 * 2 + (c + dc) % 2
        pairs.append((device, band * PATCHES + patch))
    return pairs


def plane(db, dp):
    return [
        (b * PATCHES + p, (b + db) % BANDS * PATCHES + (p + dp) % PATCHES)
        for b in range(BANDS)
        for p in range(PATCHES)
    ]


def send(values, pairs):
    return lax.ppermute(values, AXES, pairs)


def dot(a, b):
    return jnp.dot(a, b, preferred_element_type=F32)


def silu(v):
    half = 0.5 * v
    return half + half * jnp.tanh(half)


def layer_norm(v):
    centred = v - jnp.mean(v, axis=-1, keepdims=True)
    spread = jnp.mean(centred * centred, axis=-1, keepdims=True)
    return centred * lax.rsqrt(spread + epsilon)


def column(row):
    return jnp.transpose(jnp.broadcast_to(row, (8, row.shape[1])))[:, :1]


def pick_rows(row, count):
    col = column(row)
    lanes = lax.broadcasted_iota(jnp.int32, (row.shape[1], count), 1)
    return jnp.where(lanes == col, 1.0, 0.0).astype(BF16)


def add_rows(row, count):
    nodes = lax.broadcasted_iota(jnp.int32, (count, row.shape[1]), 0)
    return jnp.where(nodes == row, 1.0, 0.0).astype(BF16)


def weight(k):
    return pl.BlockSpec((None, D, D), lambda i: (k, 0, 0))


SMEM = pl.BlockSpec(memory_space=pltpu.SMEM)
VMEM = pl.BlockSpec(memory_space=pltpu.VMEM)
HBM = pl.BlockSpec(memory_space=pltpu.HBM)
ANY = pl.BlockSpec(memory_space=pl.ANY)


def stay(values):
    return pltpu.with_memory_space_constraint(values, pltpu.HBM)


class Fetched:
    def __init__(self, source, target, sem):
        self.copy, self.target, self.ready = pltpu.make_async_copy(source, target, sem), target, False
        self.copy.start()

    def __call__(self):
        if not self.ready:
            self.copy.wait()
            self.ready = True
        return self.target


def whole(shape):
    return pl.BlockSpec(shape, lambda i: (0,) * len(shape))


def params(mb):
    return pltpu.CompilerParams(
        dimension_semantics=("arbitrary",), vmem_limit_bytes=mb << 20
    )


def cost(rows, nbytes):
    return pl.CostEstimate(flops=2 * rows * D * D, bytes_accessed=nbytes, transcendentals=0)


def split_patch():
    band, patch = lax.axis_index("band"), lax.axis_index("patch")
    return band >> 2, band & 3, patch >> 1, patch & 1


def cell_index(sender):
    i = jnp.floor((sender.astype(F32) + 0.5) * (1.0 / 260)).astype(jnp.int32)
    j = sender - i * 260
    west, east = 2048 + i * 2 + j, 2064 - 258 + i * 2 + j
    return jnp.where(j < 2, west, jnp.where(j < 258, i * 256 + j - 2, east))


def near_index(sender, my_c):
    q, r = sender >> 8, sender & 255
    row = (q >= 3).astype(jnp.int32) + (q >= 6).astype(jnp.int32)
    col = q - 3 * row
    middle = jnp.where(row == 0, 0, jnp.where(row == 1, 64, 320))
    aside = jnp.where(col == 2 - 2 * my_c, 384, 576) + row * 64
    return jnp.where(col == 1, middle, aside) + r


def mesh_index(sender):
    my_y, my_z, my_x, my_c = split_patch()
    far = sender - 2304
    y, z, x, c, node = far >> 9, (far >> 7) & 3, (far >> 5) & 3, (far >> 4) & 1, far & 15
    kx, kz, kc = (my_x - x) & 3, (my_z - z) & 3, (my_c - c) & 1
    behind = jnp.where(my_z == 0, -1, 0)
    beyond = jnp.where(my_z == 3, 1, 0)
    turn = jnp.where(kz == 1, behind, jnp.where(kz == 3, beyond, 0))
    ky = (my_y - y + turn) & 3
    ky, kz = (jnp.where(k < 2, k, 5 - k) for k in (ky, kz))
    at = kc * 1024 + ky * 256 + kx * 64 + kz * 16 + node
    return jnp.where(sender < 2304, 2048 + near_index(sender, my_c), at)


def grid_body(blocks, x_ref, w0, w7, w8, sent, nxt, live):
    alive = blocks[lax.axis_index("band"), lax.axis_index("patch")] * 128
    live[...] = jnp.full(live.shape, alive, jnp.int32)
    x = x_ref[...]
    sent[...] = dot(x, w0[...]).astype(BF16)
    hidden = silu(dot(x, w7[...])).astype(BF16)
    nxt[...] = (x.astype(F32) + layer_norm(dot(hidden, w8[...]))).astype(BF16)


def grid_kernel(blocks, grid_flat, enc_w):
    blk = pl.BlockSpec((512, D), lambda i: (i, 0))
    return pl.pallas_call(
        grid_body,
        grid=(2,),
        in_specs=[SMEM, blk, weight(0), weight(7), weight(8)],
        out_specs=[blk] * 2 + [whole((8, 128))],
        out_shape=[jax.ShapeDtypeStruct((1024, D), BF16)] * 2
        + [jax.ShapeDtypeStruct((8, 128), jnp.int32)],
        compiler_params=params(60),
        cost_estimate=cost(5000, 5 << 20),
        name="grid_cells",
    )(blocks, grid_flat, *[enc_w] * 3)


def lead_body(feat, cells, d1, w2, w4, before, self_part):
    g = cells[...]
    recv = dot(g, d1[...]).astype(BF16).astype(F32)
    self_part[...] = dot(g, w4[...])
    for k in range(3):
        before[k] = (dot(feat[k], w2[...]) + recv).astype(before.dtype)


def lead_kernel(feats, grid_next, dec_w):
    lat, lon = feats.shape[1:3]
    blk = pl.BlockSpec((lon, D), lambda i: (i, 0))
    edges = pl.BlockSpec((3, None, lon, D), lambda i: (0, i, 0, 0))
    return pl.pallas_call(
        lead_body,
        grid=(lat,),
        in_specs=[edges, blk, weight(1), weight(2), weight(4)],
        out_specs=[edges, blk],
        out_shape=[
            jax.ShapeDtypeStruct(feats.shape, BF16),
            jax.ShapeDtypeStruct(grid_next.shape, F32),
        ],
        compiler_params=params(60),
        cost_estimate=cost(8000, 10 << 20),
        name="decoder_lead",
    )(feats, grid_next, *[dec_w] * 3)


def edge_sum(before, hidden_weight, target):
    hidden = silu(before).astype(BF16)
    message = layer_norm(dot(hidden, hidden_weight)).astype(BF16)
    return dot(add_rows(target, 256), message)


def node_update(m, total, w4, w5, w6):
    hid = silu(dot(m, w4()[...]) + dot(total.astype(BF16), w5()[...])).astype(BF16)
    return (m.astype(F32) + layer_norm(dot(hid, w6()[...]))).astype(BF16)


def enc_body(
    live, snd, rcv, feat, own, top, bottom, west, east, mesh_ref, enc_w, proc_w,
    nxt, psend, precv, both, rim, coarse,
    table, feat_v, rim_v, side_v, mesh_v, weights, index, live_v, sems,
):
    count = iter(range(sems.shape[0]))

    def fetch(source, target):
        return Fetched(source, target, sems.at[next(count)])

    steps = feat.shape[0] // EDGE_BLOCK
    w0 = fetch(enc_w.at[0], weights.at[0])
    rims = [fetch(top, rim_v.at[0]), fetch(bottom, rim_v.at[1])]
    sides = [fetch(v, side_v.at[pl.ds(16 * k, 16)]) for k, v in enumerate((west, east))]
    mesh = fetch(mesh_ref, mesh_v)
    w1 = fetch(enc_w.at[1], weights.at[1])
    mine = fetch(own, table.at[pl.ds(512, 1024)])
    w2, w3 = (fetch(enc_w.at[k], weights.at[k]) for k in (2, 3))
    feats = [fetch(snd, index.at[0]), fetch(rcv, index.at[1]), fetch(live, live_v)]
    for k in range(steps):
        rows = pl.ds(k * EDGE_BLOCK, EDGE_BLOCK)
        feats.append(fetch(feat.at[rows], feat_v.at[rows]))
    w4, w5, w6 = (fetch(enc_w.at[k], weights.at[k]) for k in (4, 5, 6))
    p0, p1 = (fetch(proc_w.at[k], weights.at[7 + k]) for k in (0, 1))

    table[2080:2176] = jnp.zeros((96, D), BF16)
    table[0:512] = dot(rims[0]()[...], w0()[...]).astype(BF16)
    table[1536:2048] = dot(rims[1]()[...], w0()[...]).astype(BF16)
    sides[0](), sides[1]()
    table[2048:2080] = dot(side_v[...], w0()[...]).astype(BF16)
    table[2176:2432] = dot(mesh()[...], w1()[...]).astype(BF16)
    mine()
    for ready in (w2, w3, *feats):
        ready()
    alive = live_v[0:1, 0:1]

    def edges(k, total):
        at = pl.ds(pl.multiple_of(k * EDGE_BLOCK, EDGE_BLOCK), EDGE_BLOCK)
        receiver = index[1, 0, :, at]
        sender = cell_index(index[0, 0, :, at])
        ones = jnp.concatenate([pick_rows(sender, 2176), pick_rows(receiver, 256)], axis=1)
        x = feat_v[at]
        before = dot(x, w2()[...]) + dot(ones, table[...])
        edge = k * EDGE_BLOCK + lax.broadcasted_iota(jnp.int32, (1, EDGE_BLOCK), 1)
        return total + edge_sum(before, w3()[...], jnp.where(edge < alive, receiver, -1))

    total = lax.fori_loop(0, steps, edges, jnp.zeros((256, D), F32))
    new = node_update(mesh()[...], total, w4, w5, w6)
    sent = dot(new, p0()[...]).astype(BF16)
    psend[...] = sent
    both[0:64], both[64:80] = sent[0:64], sent[240:256]
    coarse[...], rim[...] = sent[240:256], sent[0:64]
    nxt[...] = new
    precv[...] = dot(new, p1()[...]).astype(BF16)


def enc_kernel(live, senders, receivers, feats, own, top, bottom, west, east, mesh_flat, enc_w, proc_w):
    node = jax.ShapeDtypeStruct((256, D), BF16)
    return pl.pallas_call(
        enc_body,
        in_specs=[HBM] * 5 + [ANY] * 4 + [HBM] * 3,
        out_specs=[VMEM] * 6,
        out_shape=[node] * 3
        + [jax.ShapeDtypeStruct((rows, D), BF16) for rows in (80, 64, 16)],
        scratch_shapes=[
            pltpu.VMEM((2432, D), BF16),
            pltpu.VMEM(feats.shape, BF16),
            pltpu.VMEM((2, 512, D), BF16),
            pltpu.VMEM((32, D), BF16),
            pltpu.VMEM((256, D), BF16),
            pltpu.VMEM((9, D, D), BF16),
            pltpu.VMEM((2, *senders.shape), jnp.int32),
            pltpu.VMEM((8, 128), jnp.int32),
            pltpu.SemaphoreType.DMA((21,)),
        ],
        compiler_params=pltpu.CompilerParams(vmem_limit_bytes=36 << 20),
        cost_estimate=cost(25000, 10 << 20),
        name="encoder_edges",
    )(
        stay(live), stay(senders), stay(receivers), stay(feats), stay(own), top, bottom, west, east,
        stay(mesh_flat), stay(enc_w), stay(proc_w),
    )


COARSE = ((0, 256), (256, 256), (512, 256), (768, 128), (896, 128))
NEAR = ((2048, 64), (2112, 256), (2368, 64), (2432, 192), (2624, 192))


def proc_body(*refs):
    snd, rcv, feat = refs[:3]
    pieces, (recv, mesh_ref, proc_w, dec_w) = refs[3:18], refs[18:22]
    dsend, rim, table, feat_v, mesh_v, weights, index, sems = refs[22:]
    count = iter(range(sems.shape[0]))

    def fetch(source, target):
        return Fetched(source, target, sems.at[next(count)])

    places = COARSE + tuple((at + 1024, rows) for at, rows in COARSE) + NEAR
    first = [fetch(recv, table.at[pl.ds(2816, 256)])]
    for piece, (at, rows) in zip(pieces, places):
        first.append(fetch(piece.at[pl.ds(0, rows)], table.at[pl.ds(at, rows)]))
    first += [fetch(proc_w.at[k], weights.at[k - 2]) for k in (2, 3)]
    first += [fetch(feat, feat_v), fetch(snd, index.at[0]), fetch(rcv, index.at[1])]
    mesh = fetch(mesh_ref, mesh_v)
    w4, w5, w6 = (fetch(proc_w.at[k], weights.at[k - 2]) for k in (4, 5, 6))
    d0 = fetch(dec_w.at[0], weights.at[5])
    for ready in first:
        ready()

    def edges(k, total):
        at = pl.ds(pl.multiple_of(k * EDGE_BLOCK, EDGE_BLOCK), EDGE_BLOCK)
        receiver = index[1, 0, :, at]
        sender = mesh_index(index[0, 0, :, at])
        ones = jnp.concatenate([pick_rows(sender, 2816), pick_rows(receiver, 256)], axis=1)
        x = feat_v[at]
        before = dot(x, weights[0]) + dot(ones, table[...])
        return total + edge_sum(before, weights[1], receiver)

    total = lax.fori_loop(0, feat.shape[0] // EDGE_BLOCK, edges, jnp.zeros((256, D), F32))
    new = node_update(mesh()[...], total, w4, w5, w6)
    sent = dot(new, d0()[...]).astype(BF16)
    dsend[...] = sent
    rim[...] = sent[0:64]


def proc_kernel(feats, senders, receivers, pieces, recv, mesh_next, proc_w, dec_w):
    return pl.pallas_call(
        proc_body,
        in_specs=[HBM] * 3 + [ANY] * 15 + [HBM] * 4,
        out_specs=[VMEM] * 2,
        out_shape=[jax.ShapeDtypeStruct((256, D), BF16), jax.ShapeDtypeStruct((64, D), BF16)],
        scratch_shapes=[
            pltpu.VMEM((3072, D), BF16),
            pltpu.VMEM(feats.shape, BF16),
            pltpu.VMEM((256, D), BF16),
            pltpu.VMEM((6, D, D), BF16),
            pltpu.VMEM((2, *senders.shape), jnp.int32),
            pltpu.SemaphoreType.DMA((26,)),
        ],
        compiler_params=pltpu.CompilerParams(vmem_limit_bytes=36 << 20),
        cost_estimate=cost(25000, 10 << 20),
        name="mesh_edges",
    )(
        stay(senders), stay(receivers), stay(feats), *pieces, stay(recv), stay(mesh_next),
        stay(proc_w), stay(dec_w),
    )


def dec_body(snd, lead, above, own, below, beside, across, cells, self_part, w3, w5, w6, out, near):
    @pl.when(pl.program_id(0) == 0)
    def _():
        near[0:64] = above[...]
        near[64:320] = own[...]
        near[320:384] = below[...]
        near[384:576] = beside[...]
        near[576:768] = across[...]

    n = cells.shape[0]
    my_c = lax.axis_index("patch") & 1
    row = pl.ds(pl.program_id(0), 1)
    ones = [pick_rows(near_index(snd[k, row], my_c), 768) for k in range(3)]
    ones = jnp.concatenate(ones, axis=0)
    before = lead[...].astype(F32).reshape(3 * n, D) + dot(ones, near[...])
    hidden = silu(before).astype(BF16)
    message = layer_norm(dot(hidden, w3[...])).astype(BF16).astype(F32).reshape(3, n, D)
    summed = message[0] + message[1] + message[2]
    hid = silu(self_part[...] + dot(summed.astype(BF16), w5[...])).astype(BF16)
    out[...] = (cells[...].astype(F32) + layer_norm(dot(hid, w6[...]))).astype(BF16)


def dec_kernel(lead, senders, near, grid_next, self_part, dec_w):
    lat, lon = senders.shape[1:]
    blk = pl.BlockSpec((lon, D), lambda i: (i, 0))
    return pl.pallas_call(
        dec_body,
        grid=(lat,),
        in_specs=[
            whole(senders.shape),
            pl.BlockSpec((3, None, lon, D), lambda i: (0, i, 0, 0)),
        ]
        + [whole(rows.shape) for rows in near]
        + [blk, blk, weight(3), weight(5), weight(6)],
        out_specs=blk,
        out_shape=jax.ShapeDtypeStruct((lat * lon, D), BF16),
        scratch_shapes=[pltpu.VMEM((768, D), BF16)],
        compiler_params=params(36),
        cost_estimate=cost(15000, 9 << 20),
        name="decoder_edges",
    )(senders, lead, *near, grid_next, self_part, *[dec_w] * 3)


SWAP = [(d, d ^ 1) for d in range(BANDS * PATCHES)]
CROSS = [
    (d, d // PATCHES * PATCHES + (d % PATCHES + (1 if d % 2 else -1)) % PATCHES)
    for d in range(BANDS * PATCHES)
]


def mesh_rows(own, both, rim, rows, lead):
    above, below = send(both, plane(1, 0)), send(both, plane(-1, 0))
    rows = jnp.concatenate([rows, above[64:], below[64:], send(rows, torus(dz=2))], axis=0)
    third, second, first = lax.optimization_barrier([send(rows, torus(dx=k)) for k in (3, 2, 1)])
    here = jnp.concatenate([rows, first, second, third], axis=0)
    below, above, here, given = lax.optimization_barrier((below, above, here, lead[0]))
    col = jnp.concatenate([above[:64], rim, below[:64]], axis=0)
    across, beside = lax.optimization_barrier((send(col, CROSS), send(col, SWAP)))
    lead = lead[1](given)
    ahead, behind = send(here, torus(dy=1)), send(here, torus(dy=-1))
    behind, ahead, lead = lax.optimization_barrier((behind, ahead, lead))
    high, low = lax.optimization_barrier(
        (send(behind[128:], torus(dy=-1)), send(ahead[:128], torus(dy=1)))
    )
    far = low, high
    coarse = [here, ahead, behind, *far]
    return coarse + [send(v, SWAP) for v in coarse] + [above, own, below, beside, across], lead


def near_rows(own, rim):
    above, below = send(rim, plane(1, 0)), send(rim, plane(-1, 0))
    col = jnp.concatenate([above, rim, below], axis=0)
    across, beside = lax.optimization_barrier((send(col, CROSS), send(col, SWAP)))
    return above, own, below, beside, across


def shards(
    grid_state,
    mesh_state,
    g2m_features,
    g2m_sender,
    g2m_receiver,
    g2m_blocks,
    proc_features,
    proc_sender,
    proc_receiver,
    dec_features,
    dec_sender,
    enc_weights,
    proc_weights,
    dec_weights,
):
    cells = grid_state.reshape(1024, D)
    nodes = mesh_state.reshape(256, D)
    top = send(grid_state[2:4], plane(1, 0))
    bottom = send(grid_state[0:2], plane(-1, 0))
    grid_send, grid_next, live = grid_kernel(g2m_blocks, cells, enc_weights)
    bottom, top, grid_send = lax.optimization_barrier((bottom, top, grid_send))
    first = jnp.concatenate([top[:, :2], grid_state[:, :2], bottom[:, :2]], axis=0)
    final = jnp.concatenate([top[:, 254:], grid_state[:, 254:], bottom[:, 254:]], axis=0)
    west = send(final.reshape(16, D), plane(0, 1))
    east = send(first.reshape(16, D), plane(0, -1))

    mesh_next, proc_send, proc_recv, both, rim, coarse = enc_kernel(
        live, g2m_sender, g2m_receiver, g2m_features.reshape(-1, D),
        grid_send, top.reshape(512, D), bottom.reshape(512, D), west, east, nodes,
        enc_weights, proc_weights,
    )
    pieces, (lead, self_part) = mesh_rows(
        proc_send, both, rim, coarse, (grid_next, lambda g: lead_kernel(dec_features, g, dec_weights))
    )
    dec_send, rim = proc_kernel(
        proc_features.reshape(-1, D), proc_sender, proc_receiver, pieces, proc_recv,
        mesh_next, proc_weights, dec_weights,
    )
    out = dec_kernel(
        lead, dec_sender, near_rows(dec_send, rim), grid_next, self_part, dec_weights
    )
    return out.reshape(grid_state.shape)


def solution(mesh):
    placed = (
        P("band", "patch", None),
        P("band", "patch", None, None),
        P("band", "patch", None, None),
        P("band", "patch", None),
        P("band", "patch", None),
        P(),
        P("band", "patch", None, None),
        P("band", "patch", None),
        P("band", "patch", None),
        P(None, "band", "patch", None),
        P(None, "band", "patch"),
        P(),
        P(),
        P(),
    )
    return jax.shard_map(
        shards, mesh=mesh, in_specs=placed, out_specs=P("band", "patch", None), check_vma=False
    )
```

```python
import jax
import jax.numpy as jnp
from jax import lax
from jax.experimental import pallas as pl
from jax.experimental.pallas import tpu as pltpu
from jax.sharding import PartitionSpec as P

D = 512
AXES = ("band", "patch")
BANDS, PATCHES = 16, 8
EDGE_BLOCK = 1024
epsilon = 1e-05
F32, BF16 = jnp.float32, jnp.bfloat16


def split(device):
    band, patch = device // PATCHES, device % PATCHES
    return band // 4, band % 4, patch // 2, patch % 2


def torus(dy=0, dz=0, dx=0, dc=0):
    pairs = []
    for device in range(BANDS * PATCHES):
        y, z, x, c = split(device)
        band = (y + dy) % 4 * 4 + (z + dz) % 4
        patch = (x + dx) % 4 * 2 + (c + dc) % 2
        pairs.append((device, band * PATCHES + patch))
    return pairs


def plane(db, dp):
    return [
        (b * PATCHES + p, (b + db) % BANDS * PATCHES + (p + dp) % PATCHES)
        for b in range(BANDS)
        for p in range(PATCHES)
    ]


def send(values, pairs):
    return lax.ppermute(values, AXES, pairs)


def dot(a, b):
    return jnp.dot(a, b, preferred_element_type=F32)


def silu(v):
    half = 0.5 * v
    return half + half * jnp.tanh(half)


def layer_norm(v):
    centred = v - jnp.mean(v, axis=-1, keepdims=True)
    spread = jnp.mean(centred * centred, axis=-1, keepdims=True)
    return centred * lax.rsqrt(spread + epsilon)


def column(row):
    return jnp.transpose(jnp.broadcast_to(row, (8, row.shape[1])))[:, :1]


def pick_rows(row, count):
    col = column(row)
    lanes = lax.broadcasted_iota(jnp.int32, (row.shape[1], count), 1)
    return jnp.where(lanes == col, 1.0, 0.0).astype(BF16)


def add_rows(row, count):
    nodes = lax.broadcasted_iota(jnp.int32, (count, row.shape[1]), 0)
    return jnp.where(nodes == row, 1.0, 0.0).astype(BF16)


def weight(k):
    return pl.BlockSpec((None, D, D), lambda i: (k, 0, 0))


SMEM = pl.BlockSpec(memory_space=pltpu.SMEM)
VMEM = pl.BlockSpec(memory_space=pltpu.VMEM)
HBM = pl.BlockSpec(memory_space=pltpu.HBM)
ANY = pl.BlockSpec(memory_space=pl.ANY)


def stay(values):
    return pltpu.with_memory_space_constraint(values, pltpu.HBM)


def fetch_rows(fetch, source, target, rows=256):
    parts = [pl.ds(at, rows) for at in range(0, source.shape[0], rows)]
    return [fetch(source.at[part], target.at[part]) for part in parts]


class Fetched:
    def __init__(self, source, target, sem):
        self.copy, self.target, self.ready = pltpu.make_async_copy(source, target, sem), target, False
        self.copy.start()

    def __call__(self):
        if not self.ready:
            self.copy.wait()
            self.ready = True
        return self.target


def whole(shape):
    return pl.BlockSpec(shape, lambda i: (0,) * len(shape))


def params(mb):
    return pltpu.CompilerParams(
        dimension_semantics=("arbitrary",), vmem_limit_bytes=mb << 20
    )


def cost(rows, nbytes):
    return pl.CostEstimate(flops=2 * rows * D * D, bytes_accessed=nbytes, transcendentals=0)


def split_patch():
    band, patch = lax.axis_index("band"), lax.axis_index("patch")
    return band >> 2, band & 3, patch >> 1, patch & 1


def cell_index(sender):
    i = jnp.floor((sender.astype(F32) + 0.5) * (1.0 / 260)).astype(jnp.int32)
    j = sender - i * 260
    west, east = 2048 + i * 2 + j, 2064 - 258 + i * 2 + j
    return jnp.where(j < 2, west, jnp.where(j < 258, i * 256 + j - 2, east))


def near_index(sender, my_c):
    q, r = sender >> 8, sender & 255
    row = (q >= 3).astype(jnp.int32) + (q >= 6).astype(jnp.int32)
    col = q - 3 * row
    middle = jnp.where(row == 0, 0, jnp.where(row == 1, 64, 320))
    aside = jnp.where(col == 2 - 2 * my_c, 384, 576) + row * 64
    return jnp.where(col == 1, middle, aside) + r


def mesh_index(sender):
    my_y, my_z, my_x, my_c = split_patch()
    far = sender - 2304
    y, z, x, c, node = far >> 9, (far >> 7) & 3, (far >> 5) & 3, (far >> 4) & 1, far & 15
    kx, kz, kc = (my_x - x) & 3, (my_z - z) & 3, (my_c - c) & 1
    behind = jnp.where(my_z == 0, -1, 0)
    beyond = jnp.where(my_z == 3, 1, 0)
    turn = jnp.where(kz == 1, behind, jnp.where(kz == 3, beyond, 0))
    ky = (my_y - y + turn) & 3
    ky, kz = (jnp.where(k < 2, k, 5 - k) for k in (ky, kz))
    at = kc * 1024 + ky * 256 + kx * 64 + kz * 16 + node
    return jnp.where(sender < 2304, 2048 + near_index(sender, my_c), at)


def grid_body(blocks, x_ref, w0, w7, w8, sent, nxt, live):
    alive = blocks[lax.axis_index("band"), lax.axis_index("patch")] * 128
    live[...] = jnp.full(live.shape, alive, jnp.int32)
    x = x_ref[...]
    sent[...] = dot(x, w0[...]).astype(BF16)
    hidden = silu(dot(x, w7[...])).astype(BF16)
    nxt[...] = (x.astype(F32) + layer_norm(dot(hidden, w8[...]))).astype(BF16)


def grid_kernel(blocks, grid_flat, enc_w):
    blk = pl.BlockSpec((512, D), lambda i: (i, 0))
    return pl.pallas_call(
        grid_body,
        grid=(2,),
        in_specs=[SMEM, blk, weight(0), weight(7), weight(8)],
        out_specs=[blk] * 2 + [whole((8, 128))],
        out_shape=[jax.ShapeDtypeStruct((1024, D), BF16)] * 2
        + [jax.ShapeDtypeStruct((8, 128), jnp.int32)],
        compiler_params=params(60),
        cost_estimate=cost(5000, 5 << 20),
        name="grid_cells",
    )(blocks, grid_flat, *[enc_w] * 3)


def lead_body(feat, cells, d1, w2, w4, before, self_part):
    g = cells[...]
    recv = dot(g, d1[...]).astype(BF16).astype(F32)
    self_part[...] = dot(g, w4[...])
    for k in range(3):
        before[k] = (dot(feat[k], w2[...]) + recv).astype(before.dtype)


def lead_kernel(feats, grid_next, dec_w):
    lat, lon = feats.shape[1:3]
    blk = pl.BlockSpec((lon, D), lambda i: (i, 0))
    edges = pl.BlockSpec((3, None, lon, D), lambda i: (0, i, 0, 0))
    return pl.pallas_call(
        lead_body,
        grid=(lat,),
        in_specs=[edges, blk, weight(1), weight(2), weight(4)],
        out_specs=[edges, blk],
        out_shape=[
            jax.ShapeDtypeStruct(feats.shape, BF16),
            jax.ShapeDtypeStruct(grid_next.shape, F32),
        ],
        compiler_params=params(60),
        cost_estimate=cost(8000, 10 << 20),
        name="decoder_lead",
    )(feats, grid_next, *[dec_w] * 3)


def edge_sum(before, hidden_weight, target):
    hidden = silu(before).astype(BF16)
    message = layer_norm(dot(hidden, hidden_weight)).astype(BF16)
    return dot(add_rows(target, 256), message)


def node_update(m, total, w4, w5, w6):
    hid = silu(dot(m, w4()[...]) + dot(total.astype(BF16), w5()[...])).astype(BF16)
    return (m.astype(F32) + layer_norm(dot(hid, w6()[...]))).astype(BF16)


def enc_body(
    live, snd, rcv, feat, own, top, bottom, west, east, mesh_ref, enc_w, proc_w,
    nxt, psend, precv, both, rim, coarse,
    table, feat_v, rim_v, side_v, mesh_v, weights, index, live_v, sems,
):
    count = iter(range(sems.shape[0]))

    def fetch(source, target):
        return Fetched(source, target, sems.at[next(count)])

    steps = feat.shape[0] // EDGE_BLOCK
    w0 = fetch(enc_w.at[0], weights.at[0])
    rims = [fetch(top, rim_v.at[0]), fetch(bottom, rim_v.at[1])]
    sides = [fetch(v, side_v.at[pl.ds(16 * k, 16)]) for k, v in enumerate((west, east))]
    mesh = fetch(mesh_ref, mesh_v)
    w1 = fetch(enc_w.at[1], weights.at[1])
    mine = fetch_rows(fetch, own, table.at[pl.ds(512, 1024)])
    w2, w3 = (fetch(enc_w.at[k], weights.at[k]) for k in (2, 3))
    feats = [fetch(snd, index.at[0]), fetch(rcv, index.at[1]), fetch(live, live_v)]
    feats += fetch_rows(fetch, feat, feat_v)
    w4, w5, w6 = (fetch(enc_w.at[k], weights.at[k]) for k in (4, 5, 6))
    p0, p1 = (fetch(proc_w.at[k], weights.at[7 + k]) for k in (0, 1))

    table[2080:2176] = jnp.zeros((96, D), BF16)
    table[0:512] = dot(rims[0]()[...], w0()[...]).astype(BF16)
    table[1536:2048] = dot(rims[1]()[...], w0()[...]).astype(BF16)
    sides[0](), sides[1]()
    table[2048:2080] = dot(side_v[...], w0()[...]).astype(BF16)
    table[2176:2432] = dot(mesh()[...], w1()[...]).astype(BF16)
    for ready in mine:
        ready()
    for ready in (w2, w3, *feats):
        ready()
    alive = live_v[0:1, 0:1]

    def edges(k, total):
        at = pl.ds(pl.multiple_of(k * EDGE_BLOCK, EDGE_BLOCK), EDGE_BLOCK)
        receiver = index[1, 0, :, at]
        sender = cell_index(index[0, 0, :, at])
        ones = jnp.concatenate([pick_rows(sender, 2176), pick_rows(receiver, 256)], axis=1)
        x = feat_v[at]
        before = dot(x, w2()[...]) + dot(ones, table[...])
        edge = k * EDGE_BLOCK + lax.broadcasted_iota(jnp.int32, (1, EDGE_BLOCK), 1)
        return total + edge_sum(before, w3()[...], jnp.where(edge < alive, receiver, -1))

    total = lax.fori_loop(0, steps, edges, jnp.zeros((256, D), F32))
    new = node_update(mesh()[...], total, w4, w5, w6)
    sent = dot(new, p0()[...]).astype(BF16)
    psend[...] = sent
    both[0:64], both[64:80] = sent[0:64], sent[240:256]
    coarse[...], rim[...] = sent[240:256], sent[0:64]
    nxt[...] = new
    precv[...] = dot(new, p1()[...]).astype(BF16)


def enc_kernel(live, senders, receivers, feats, own, top, bottom, west, east, mesh_flat, enc_w, proc_w):
    node = jax.ShapeDtypeStruct((256, D), BF16)
    return pl.pallas_call(
        enc_body,
        in_specs=[HBM] * 5 + [ANY] * 4 + [HBM] * 3,
        out_specs=[VMEM] * 6,
        out_shape=[node] * 3
        + [jax.ShapeDtypeStruct((rows, D), BF16) for rows in (80, 64, 16)],
        scratch_shapes=[
            pltpu.VMEM((2432, D), BF16),
            pltpu.VMEM(feats.shape, BF16),
            pltpu.VMEM((2, 512, D), BF16),
            pltpu.VMEM((32, D), BF16),
            pltpu.VMEM((256, D), BF16),
            pltpu.VMEM((9, D, D), BF16),
            pltpu.VMEM((2, *senders.shape), jnp.int32),
            pltpu.VMEM((8, 128), jnp.int32),
            pltpu.SemaphoreType.DMA((32,)),
        ],
        compiler_params=pltpu.CompilerParams(vmem_limit_bytes=36 << 20),
        cost_estimate=cost(25000, 10 << 20),
        name="encoder_edges",
    )(
        stay(live), stay(senders), stay(receivers), stay(feats), stay(own), top, bottom, west, east,
        stay(mesh_flat), stay(enc_w), stay(proc_w),
    )


COARSE = ((0, 256), (256, 256), (512, 256), (768, 128), (896, 128))
NEAR = ((2048, 64), (2112, 256), (2368, 64), (2432, 192), (2624, 192))


def proc_body(*refs):
    snd, rcv, feat = refs[:3]
    pieces, (recv, mesh_ref, proc_w, dec_w) = refs[3:18], refs[18:22]
    dsend, rim, table, feat_v, mesh_v, weights, index, sems = refs[22:]
    count = iter(range(sems.shape[0]))

    def fetch(source, target):
        return Fetched(source, target, sems.at[next(count)])

    places = COARSE + tuple((at + 1024, rows) for at, rows in COARSE) + NEAR
    first = [fetch(snd, index.at[0]), fetch(rcv, index.at[1]), fetch(recv, table.at[pl.ds(2816, 256)])]
    first += [fetch(proc_w.at[k], weights.at[k - 2]) for k in (2, 3)]
    first += fetch_rows(fetch, feat, feat_v)
    for piece, (at, rows) in zip(pieces, places):
        first.append(fetch(piece.at[pl.ds(0, rows)], table.at[pl.ds(at, rows)]))
    mesh = fetch(mesh_ref, mesh_v)
    w4, w5, w6 = (fetch(proc_w.at[k], weights.at[k - 2]) for k in (4, 5, 6))
    d0 = fetch(dec_w.at[0], weights.at[5])
    for ready in first:
        ready()

    def edges(k, total):
        at = pl.ds(pl.multiple_of(k * EDGE_BLOCK, EDGE_BLOCK), EDGE_BLOCK)
        receiver = index[1, 0, :, at]
        sender = mesh_index(index[0, 0, :, at])
        ones = jnp.concatenate([pick_rows(sender, 2816), pick_rows(receiver, 256)], axis=1)
        x = feat_v[at]
        before = dot(x, weights[0]) + dot(ones, table[...])
        return total + edge_sum(before, weights[1], receiver)

    total = lax.fori_loop(0, feat.shape[0] // EDGE_BLOCK, edges, jnp.zeros((256, D), F32))
    new = node_update(mesh()[...], total, w4, w5, w6)
    sent = dot(new, d0()[...]).astype(BF16)
    dsend[...] = sent
    rim[...] = sent[0:64]


def proc_kernel(feats, senders, receivers, pieces, recv, mesh_next, proc_w, dec_w):
    return pl.pallas_call(
        proc_body,
        in_specs=[HBM] * 3 + [ANY] * 15 + [HBM] * 4,
        out_specs=[VMEM] * 2,
        out_shape=[jax.ShapeDtypeStruct((256, D), BF16), jax.ShapeDtypeStruct((64, D), BF16)],
        scratch_shapes=[
            pltpu.VMEM((3072, D), BF16),
            pltpu.VMEM(feats.shape, BF16),
            pltpu.VMEM((256, D), BF16),
            pltpu.VMEM((6, D, D), BF16),
            pltpu.VMEM((2, *senders.shape), jnp.int32),
            pltpu.SemaphoreType.DMA((34,)),
        ],
        compiler_params=pltpu.CompilerParams(vmem_limit_bytes=36 << 20),
        cost_estimate=cost(25000, 10 << 20),
        name="mesh_edges",
    )(
        stay(senders), stay(receivers), stay(feats), *pieces, stay(recv), stay(mesh_next),
        stay(proc_w), stay(dec_w),
    )


def dec_body(snd, lead, above, own, below, beside, across, cells, self_part, w3, w5, w6, out, near):
    @pl.when(pl.program_id(0) == 0)
    def _():
        near[0:64] = above[...]
        near[64:320] = own[...]
        near[320:384] = below[...]
        near[384:576] = beside[...]
        near[576:768] = across[...]

    n = cells.shape[0]
    my_c = lax.axis_index("patch") & 1
    row = pl.ds(pl.program_id(0), 1)
    ones = [pick_rows(near_index(snd[k, row], my_c), 768) for k in range(3)]
    ones = jnp.concatenate(ones, axis=0)
    before = lead[...].astype(F32).reshape(3 * n, D) + dot(ones, near[...])
    hidden = silu(before).astype(BF16)
    message = layer_norm(dot(hidden, w3[...])).astype(BF16).astype(F32).reshape(3, n, D)
    summed = message[0] + message[1] + message[2]
    hid = silu(self_part[...] + dot(summed.astype(BF16), w5[...])).astype(BF16)
    out[...] = (cells[...].astype(F32) + layer_norm(dot(hid, w6[...]))).astype(BF16)


def dec_kernel(lead, senders, near, grid_next, self_part, dec_w):
    lat, lon = senders.shape[1:]
    blk = pl.BlockSpec((lon, D), lambda i: (i, 0))
    return pl.pallas_call(
        dec_body,
        grid=(lat,),
        in_specs=[
            whole(senders.shape),
            pl.BlockSpec((3, None, lon, D), lambda i: (0, i, 0, 0)),
        ]
        + [whole(rows.shape) for rows in near]
        + [blk, blk, weight(3), weight(5), weight(6)],
        out_specs=blk,
        out_shape=jax.ShapeDtypeStruct((lat * lon, D), BF16),
        scratch_shapes=[pltpu.VMEM((768, D), BF16)],
        compiler_params=params(36),
        cost_estimate=cost(15000, 9 << 20),
        name="decoder_edges",
    )(senders, lead, *near, grid_next, self_part, *[dec_w] * 3)


SWAP = [(d, d ^ 1) for d in range(BANDS * PATCHES)]
CROSS = [
    (d, d // PATCHES * PATCHES + (d % PATCHES + (1 if d % 2 else -1)) % PATCHES)
    for d in range(BANDS * PATCHES)
]


def mesh_rows(own, both, rim, rows, lead):
    above, below = send(both, plane(1, 0)), send(both, plane(-1, 0))
    rows = jnp.concatenate([rows, above[64:], below[64:], send(rows, torus(dz=2))], axis=0)
    third, second, first = lax.optimization_barrier([send(rows, torus(dx=k)) for k in (3, 2, 1)])
    here = jnp.concatenate([rows, first, second, third], axis=0)
    below, above, here, given = lax.optimization_barrier((below, above, here, lead[0]))
    col = jnp.concatenate([above[:64], rim, below[:64]], axis=0)
    across, beside = lax.optimization_barrier((send(col, CROSS), send(col, SWAP)))
    lead = lead[1](given)
    ahead, behind = send(here, torus(dy=1)), send(here, torus(dy=-1))
    behind, ahead, lead = lax.optimization_barrier((behind, ahead, lead))
    high, low = lax.optimization_barrier(
        (send(behind[128:], torus(dy=-1)), send(ahead[:128], torus(dy=1)))
    )
    far = low, high
    coarse = [here, ahead, behind, *far]
    return coarse + [send(v, SWAP) for v in coarse] + [above, own, below, beside, across], lead


def near_rows(own, rim):
    above, below = send(rim, plane(1, 0)), send(rim, plane(-1, 0))
    col = jnp.concatenate([above, rim, below], axis=0)
    across, beside = lax.optimization_barrier((send(col, CROSS), send(col, SWAP)))
    return above, own, below, beside, across


def shards(
    grid_state,
    mesh_state,
    g2m_features,
    g2m_sender,
    g2m_receiver,
    g2m_blocks,
    proc_features,
    proc_sender,
    proc_receiver,
    dec_features,
    dec_sender,
    enc_weights,
    proc_weights,
    dec_weights,
):
    cells = grid_state.reshape(1024, D)
    nodes = mesh_state.reshape(256, D)
    top = send(grid_state[2:4], plane(1, 0))
    bottom = send(grid_state[0:2], plane(-1, 0))
    grid_send, grid_next, live = grid_kernel(g2m_blocks, cells, enc_weights)
    bottom, top, grid_send = lax.optimization_barrier((bottom, top, grid_send))
    first = jnp.concatenate([top[:, :2], grid_state[:, :2], bottom[:, :2]], axis=0)
    final = jnp.concatenate([top[:, 254:], grid_state[:, 254:], bottom[:, 254:]], axis=0)
    west = send(final.reshape(16, D), plane(0, 1))
    east = send(first.reshape(16, D), plane(0, -1))

    mesh_next, proc_send, proc_recv, both, rim, coarse = enc_kernel(
        live, g2m_sender, g2m_receiver, g2m_features.reshape(-1, D),
        grid_send, top.reshape(512, D), bottom.reshape(512, D), west, east, nodes,
        enc_weights, proc_weights,
    )
    pieces, (lead, self_part) = mesh_rows(
        proc_send, both, rim, coarse, (grid_next, lambda g: lead_kernel(dec_features, g, dec_weights))
    )
    dec_send, rim = proc_kernel(
        proc_features.reshape(-1, D), proc_sender, proc_receiver, pieces, proc_recv,
        mesh_next, proc_weights, dec_weights,
    )
    out = dec_kernel(
        lead, dec_sender, near_rows(dec_send, rim), grid_next, self_part, dec_weights
    )
    return out.reshape(grid_state.shape)


def solution(mesh):
    placed = (
        P("band", "patch", None),
        P("band", "patch", None, None),
        P("band", "patch", None, None),
        P("band", "patch", None),
        P("band", "patch", None),
        P(),
        P("band", "patch", None, None),
        P("band", "patch", None),
        P("band", "patch", None),
        P(None, "band", "patch", None),
        P(None, "band", "patch"),
        P(),
        P(),
        P(),
    )
    return jax.shard_map(
        shards, mesh=mesh, in_specs=placed, out_specs=P("band", "patch", None), check_vma=False
    )
```

```python
import jax
import jax.numpy as jnp
from jax import lax
from jax.experimental import pallas as pl
from jax.experimental.pallas import tpu as pltpu
from jax.sharding import PartitionSpec as P

D = 512
AXES = ("band", "patch")
BANDS, PATCHES = 16, 8
EDGE_BLOCK = 1024
epsilon = 1e-05
F32, BF16 = jnp.float32, jnp.bfloat16


def split(device):
    band, patch = device // PATCHES, device % PATCHES
    return band // 4, band % 4, patch // 2, patch % 2


def torus(dy=0, dz=0, dx=0, dc=0):
    pairs = []
    for device in range(BANDS * PATCHES):
        y, z, x, c = split(device)
        band = (y + dy) % 4 * 4 + (z + dz) % 4
        patch = (x + dx) % 4 * 2 + (c + dc) % 2
        pairs.append((device, band * PATCHES + patch))
    return pairs


def plane(db, dp):
    return [
        (b * PATCHES + p, (b + db) % BANDS * PATCHES + (p + dp) % PATCHES)
        for b in range(BANDS)
        for p in range(PATCHES)
    ]


def send(values, pairs):
    return lax.ppermute(values, AXES, pairs)


def dot(a, b):
    return jnp.dot(a, b, preferred_element_type=F32)


def silu(v):
    half = 0.5 * v
    return half + half * jnp.tanh(half)


def layer_norm(v):
    centred = v - jnp.mean(v, axis=-1, keepdims=True)
    spread = jnp.mean(centred * centred, axis=-1, keepdims=True)
    return centred * lax.rsqrt(spread + epsilon)


def column(row):
    return jnp.transpose(jnp.broadcast_to(row, (8, row.shape[1])))[:, :1]


def pick_rows(row, count):
    col = column(row)
    lanes = lax.broadcasted_iota(jnp.int32, (row.shape[1], count), 1)
    return jnp.where(lanes == col, 1.0, 0.0).astype(BF16)


def add_rows(row, count):
    nodes = lax.broadcasted_iota(jnp.int32, (count, row.shape[1]), 0)
    return jnp.where(nodes == row, 1.0, 0.0).astype(BF16)


def weight(k):
    return pl.BlockSpec((None, D, D), lambda i: (k, 0, 0))


SMEM = pl.BlockSpec(memory_space=pltpu.SMEM)
VMEM = pl.BlockSpec(memory_space=pltpu.VMEM)
HBM = pl.BlockSpec(memory_space=pltpu.HBM)
ANY = pl.BlockSpec(memory_space=pl.ANY)


def stay(values):
    return pltpu.with_memory_space_constraint(values, pltpu.HBM)


def fetch_rows(fetch, source, target, rows=256):
    parts = [pl.ds(at, rows) for at in range(0, source.shape[0], rows)]
    return [fetch(source.at[part], target.at[part]) for part in parts]


class Fetched:
    def __init__(self, source, target, sem):
        self.copy, self.target, self.ready = pltpu.make_async_copy(source, target, sem), target, False
        self.copy.start()

    def __call__(self):
        if not self.ready:
            self.copy.wait()
            self.ready = True
        return self.target


def whole(shape):
    return pl.BlockSpec(shape, lambda i: (0,) * len(shape))


def params(mb):
    return pltpu.CompilerParams(
        dimension_semantics=("arbitrary",), vmem_limit_bytes=mb << 20
    )


def cost(rows, nbytes):
    return pl.CostEstimate(flops=2 * rows * D * D, bytes_accessed=nbytes, transcendentals=0)


def split_patch():
    band, patch = lax.axis_index("band"), lax.axis_index("patch")
    return band >> 2, band & 3, patch >> 1, patch & 1


def cell_index(sender):
    i = jnp.floor((sender.astype(F32) + 0.5) * (1.0 / 260)).astype(jnp.int32)
    j = sender - i * 260
    west, east = 2048 + i * 2 + j, 2064 - 258 + i * 2 + j
    return jnp.where(j < 2, west, jnp.where(j < 258, i * 256 + j - 2, east))


def near_index(sender, my_c):
    q, r = sender >> 8, sender & 255
    row = (q >= 3).astype(jnp.int32) + (q >= 6).astype(jnp.int32)
    col = q - 3 * row
    middle = jnp.where(row == 0, 0, jnp.where(row == 1, 64, 320))
    aside = jnp.where(col == 2 - 2 * my_c, 384, 576) + row * 64
    return jnp.where(col == 1, middle, aside) + r


def mesh_index(sender):
    my_y, my_z, my_x, my_c = split_patch()
    far = sender - 2304
    y, z, x, c, node = far >> 9, (far >> 7) & 3, (far >> 5) & 3, (far >> 4) & 1, far & 15
    kx, kz, kc = (my_x - x) & 3, (my_z - z) & 3, (my_c - c) & 1
    behind = jnp.where(my_z == 0, -1, 0)
    beyond = jnp.where(my_z == 3, 1, 0)
    turn = jnp.where(kz == 1, behind, jnp.where(kz == 3, beyond, 0))
    ky = (my_y - y + turn) & 3
    ky, kz = (jnp.where(k < 2, k, 5 - k) for k in (ky, kz))
    at = kc * 1024 + ky * 256 + kx * 64 + kz * 16 + node
    return jnp.where(sender < 2304, 2048 + near_index(sender, my_c), at)


def grid_body(blocks, x_ref, w0, w7, w8, sent, nxt, live):
    alive = blocks[lax.axis_index("band"), lax.axis_index("patch")] * 128
    live[...] = jnp.full(live.shape, alive, jnp.int32)
    x = x_ref[...]
    sent[...] = dot(x, w0[...]).astype(BF16)
    hidden = silu(dot(x, w7[...])).astype(BF16)
    nxt[...] = (x.astype(F32) + layer_norm(dot(hidden, w8[...]))).astype(BF16)


def grid_kernel(blocks, grid_flat, enc_w):
    blk = pl.BlockSpec((512, D), lambda i: (i, 0))
    return pl.pallas_call(
        grid_body,
        grid=(2,),
        in_specs=[SMEM, blk, weight(0), weight(7), weight(8)],
        out_specs=[blk] * 2 + [whole((8, 128))],
        out_shape=[jax.ShapeDtypeStruct((1024, D), BF16)] * 2
        + [jax.ShapeDtypeStruct((8, 128), jnp.int32)],
        compiler_params=params(60),
        cost_estimate=cost(5000, 5 << 20),
        name="grid_cells",
    )(blocks, grid_flat, *[enc_w] * 3)


def lead_body(feat, cells, d1, w2, w4, before, self_part):
    g = cells[...]
    recv = dot(g, d1[...]).astype(BF16).astype(F32)
    self_part[...] = dot(g, w4[...])
    for k in range(3):
        before[k] = (dot(feat[k], w2[...]) + recv).astype(before.dtype)


def lead_kernel(feats, grid_next, dec_w):
    lat, lon = feats.shape[1:3]
    blk = pl.BlockSpec((lon, D), lambda i: (i, 0))
    edges = pl.BlockSpec((3, None, lon, D), lambda i: (0, i, 0, 0))
    return pl.pallas_call(
        lead_body,
        grid=(lat,),
        in_specs=[edges, blk, weight(1), weight(2), weight(4)],
        out_specs=[edges, blk],
        out_shape=[
            jax.ShapeDtypeStruct(feats.shape, BF16),
            jax.ShapeDtypeStruct(grid_next.shape, F32),
        ],
        compiler_params=params(24),
        cost_estimate=cost(8000, 10 << 20),
        name="decoder_lead",
    )(stay(feats), stay(grid_next), *[stay(dec_w)] * 3)


def edge_sum(before, hidden_weight, target):
    hidden = silu(before).astype(BF16)
    message = layer_norm(dot(hidden, hidden_weight)).astype(BF16)
    return dot(add_rows(target, 256), message)


def node_update(m, total, w4, w5, w6):
    hid = silu(dot(m, w4()[...]) + dot(total.astype(BF16), w5()[...])).astype(BF16)
    return (m.astype(F32) + layer_norm(dot(hid, w6()[...]))).astype(BF16)


def enc_body(
    live, snd, rcv, feat, own, top, bottom, west, east, mesh_ref, enc_w, proc_w,
    nxt, psend, precv, both, rim, coarse,
    table, feat_v, rim_v, side_v, mesh_v, weights, index, live_v, sems,
):
    count = iter(range(sems.shape[0]))

    def fetch(source, target):
        return Fetched(source, target, sems.at[next(count)])

    steps = feat.shape[0] // EDGE_BLOCK
    w0 = fetch(enc_w.at[0], weights.at[0])
    rims = [fetch(top, rim_v.at[0]), fetch(bottom, rim_v.at[1])]
    sides = [fetch(v, side_v.at[pl.ds(16 * k, 16)]) for k, v in enumerate((west, east))]
    mesh = fetch(mesh_ref, mesh_v)
    w1 = fetch(enc_w.at[1], weights.at[1])
    mine = fetch_rows(fetch, own, table.at[pl.ds(512, 1024)])
    w2, w3 = (fetch(enc_w.at[k], weights.at[k]) for k in (2, 3))
    feats = [fetch(snd, index.at[0]), fetch(rcv, index.at[1]), fetch(live, live_v)]
    feats += fetch_rows(fetch, feat, feat_v)
    w4, w5, w6 = (fetch(enc_w.at[k], weights.at[k]) for k in (4, 5, 6))
    p0, p1 = (fetch(proc_w.at[k], weights.at[7 + k]) for k in (0, 1))

    table[2080:2176] = jnp.zeros((96, D), BF16)
    table[0:512] = dot(rims[0]()[...], w0()[...]).astype(BF16)
    table[1536:2048] = dot(rims[1]()[...], w0()[...]).astype(BF16)
    sides[0](), sides[1]()
    table[2048:2080] = dot(side_v[...], w0()[...]).astype(BF16)
    table[2176:2432] = dot(mesh()[...], w1()[...]).astype(BF16)
    for ready in mine:
        ready()
    for ready in (w2, w3, *feats):
        ready()
    alive = live_v[0:1, 0:1]

    def edges(k, total):
        at = pl.ds(pl.multiple_of(k * EDGE_BLOCK, EDGE_BLOCK), EDGE_BLOCK)
        receiver = index[1, 0, :, at]
        sender = cell_index(index[0, 0, :, at])
        ones = jnp.concatenate([pick_rows(sender, 2176), pick_rows(receiver, 256)], axis=1)
        x = feat_v[at]
        before = dot(x, w2()[...]) + dot(ones, table[...])
        edge = k * EDGE_BLOCK + lax.broadcasted_iota(jnp.int32, (1, EDGE_BLOCK), 1)
        return total + edge_sum(before, w3()[...], jnp.where(edge < alive, receiver, -1))

    total = lax.fori_loop(0, steps, edges, jnp.zeros((256, D), F32))
    new = node_update(mesh()[...], total, w4, w5, w6)
    sent = dot(new, p0()[...]).astype(BF16)
    psend[...] = sent
    both[0:64], both[64:80] = sent[0:64], sent[240:256]
    coarse[...], rim[...] = sent[240:256], sent[0:64]
    nxt[...] = new
    precv[...] = dot(new, p1()[...]).astype(BF16)


def enc_kernel(live, senders, receivers, feats, own, top, bottom, west, east, mesh_flat, enc_w, proc_w):
    node = jax.ShapeDtypeStruct((256, D), BF16)
    return pl.pallas_call(
        enc_body,
        in_specs=[HBM] * 5 + [ANY] * 4 + [HBM] * 3,
        out_specs=[VMEM] * 6,
        out_shape=[node] * 3
        + [jax.ShapeDtypeStruct((rows, D), BF16) for rows in (80, 64, 16)],
        scratch_shapes=[
            pltpu.VMEM((2432, D), BF16),
            pltpu.VMEM(feats.shape, BF16),
            pltpu.VMEM((2, 512, D), BF16),
            pltpu.VMEM((32, D), BF16),
            pltpu.VMEM((256, D), BF16),
            pltpu.VMEM((9, D, D), BF16),
            pltpu.VMEM((2, *senders.shape), jnp.int32),
            pltpu.VMEM((8, 128), jnp.int32),
            pltpu.SemaphoreType.DMA((32,)),
        ],
        compiler_params=pltpu.CompilerParams(vmem_limit_bytes=36 << 20),
        cost_estimate=cost(25000, 10 << 20),
        name="encoder_edges",
    )(
        stay(live), stay(senders), stay(receivers), stay(feats), stay(own), top, bottom, west, east,
        stay(mesh_flat), stay(enc_w), stay(proc_w),
    )


COARSE = ((0, 256), (256, 256), (512, 256), (768, 128), (896, 128))
NEAR = ((2048, 64), (2112, 256), (2368, 64), (2432, 192), (2624, 192))


def proc_body(*refs):
    snd, rcv, feat = refs[:3]
    pieces, (recv, mesh_ref, proc_w, dec_w) = refs[3:18], refs[18:22]
    dsend, rim, table, feat_v, mesh_v, weights, index, sems = refs[22:]
    count = iter(range(sems.shape[0]))

    def fetch(source, target):
        return Fetched(source, target, sems.at[next(count)])

    places = COARSE + tuple((at + 1024, rows) for at, rows in COARSE) + NEAR
    first = [fetch(snd, index.at[0]), fetch(rcv, index.at[1]), fetch(recv, table.at[pl.ds(2816, 256)])]
    first += [fetch(proc_w.at[k], weights.at[k - 2]) for k in (2, 3)]
    first += fetch_rows(fetch, feat, feat_v)
    for piece, (at, rows) in zip(pieces, places):
        first.append(fetch(piece.at[pl.ds(0, rows)], table.at[pl.ds(at, rows)]))
    mesh = fetch(mesh_ref, mesh_v)
    w4, w5, w6 = (fetch(proc_w.at[k], weights.at[k - 2]) for k in (4, 5, 6))
    d0 = fetch(dec_w.at[0], weights.at[5])
    for ready in first:
        ready()

    def edges(k, total):
        at = pl.ds(pl.multiple_of(k * EDGE_BLOCK, EDGE_BLOCK), EDGE_BLOCK)
        receiver = index[1, 0, :, at]
        sender = mesh_index(index[0, 0, :, at])
        ones = jnp.concatenate([pick_rows(sender, 2816), pick_rows(receiver, 256)], axis=1)
        x = feat_v[at]
        before = dot(x, weights[0]) + dot(ones, table[...])
        return total + edge_sum(before, weights[1], receiver)

    total = lax.fori_loop(0, feat.shape[0] // EDGE_BLOCK, edges, jnp.zeros((256, D), F32))
    new = node_update(mesh()[...], total, w4, w5, w6)
    sent = dot(new, d0()[...]).astype(BF16)
    dsend[...] = sent
    rim[...] = sent[0:64]


def proc_kernel(feats, senders, receivers, pieces, recv, mesh_next, proc_w, dec_w):
    return pl.pallas_call(
        proc_body,
        in_specs=[HBM] * 3 + [ANY] * 15 + [HBM] * 4,
        out_specs=[VMEM] * 2,
        out_shape=[jax.ShapeDtypeStruct((256, D), BF16), jax.ShapeDtypeStruct((64, D), BF16)],
        scratch_shapes=[
            pltpu.VMEM((3072, D), BF16),
            pltpu.VMEM(feats.shape, BF16),
            pltpu.VMEM((256, D), BF16),
            pltpu.VMEM((6, D, D), BF16),
            pltpu.VMEM((2, *senders.shape), jnp.int32),
            pltpu.SemaphoreType.DMA((34,)),
        ],
        compiler_params=pltpu.CompilerParams(vmem_limit_bytes=36 << 20),
        cost_estimate=cost(25000, 10 << 20),
        name="mesh_edges",
    )(
        stay(senders), stay(receivers), stay(feats), *pieces, stay(recv), stay(mesh_next),
        stay(proc_w), stay(dec_w),
    )


def dec_body(snd, lead, above, own, below, beside, across, cells, self_part, w3, w5, w6, out, near):
    @pl.when(pl.program_id(0) == 0)
    def _():
        near[0:64] = above[...]
        near[64:320] = own[...]
        near[320:384] = below[...]
        near[384:576] = beside[...]
        near[576:768] = across[...]

    n = cells.shape[0]
    my_c = lax.axis_index("patch") & 1
    row = pl.ds(pl.program_id(0), 1)
    ones = [pick_rows(near_index(snd[k, row], my_c), 768) for k in range(3)]
    ones = jnp.concatenate(ones, axis=0)
    before = lead[...].astype(F32).reshape(3 * n, D) + dot(ones, near[...])
    hidden = silu(before).astype(BF16)
    message = layer_norm(dot(hidden, w3[...])).astype(BF16).astype(F32).reshape(3, n, D)
    summed = message[0] + message[1] + message[2]
    hid = silu(self_part[...] + dot(summed.astype(BF16), w5[...])).astype(BF16)
    out[...] = (cells[...].astype(F32) + layer_norm(dot(hid, w6[...]))).astype(BF16)


def dec_kernel(lead, senders, near, grid_next, self_part, dec_w):
    lat, lon = senders.shape[1:]
    blk = pl.BlockSpec((lon, D), lambda i: (i, 0))
    return pl.pallas_call(
        dec_body,
        grid=(lat,),
        in_specs=[
            whole(senders.shape),
            pl.BlockSpec((3, None, lon, D), lambda i: (0, i, 0, 0)),
        ]
        + [whole(rows.shape) for rows in near]
        + [blk, blk, weight(3), weight(5), weight(6)],
        out_specs=blk,
        out_shape=jax.ShapeDtypeStruct((lat * lon, D), BF16),
        scratch_shapes=[pltpu.VMEM((768, D), BF16)],
        compiler_params=params(36),
        cost_estimate=cost(15000, 9 << 20),
        name="decoder_edges",
    )(senders, lead, *near, grid_next, self_part, *[dec_w] * 3)


SWAP = [(d, d ^ 1) for d in range(BANDS * PATCHES)]
CROSS = [
    (d, d // PATCHES * PATCHES + (d % PATCHES + (1 if d % 2 else -1)) % PATCHES)
    for d in range(BANDS * PATCHES)
]


def mesh_rows(own, both, rim, rows, lead):
    above, below = send(both, plane(1, 0)), send(both, plane(-1, 0))
    rows = jnp.concatenate([rows, above[64:], below[64:], send(rows, torus(dz=2))], axis=0)
    third, second, first = lax.optimization_barrier([send(rows, torus(dx=k)) for k in (3, 2, 1)])
    here = jnp.concatenate([rows, first, second, third], axis=0)
    below, above, here, given = lax.optimization_barrier((below, above, here, lead[0]))
    col = jnp.concatenate([above[:64], rim, below[:64]], axis=0)
    across, beside = lax.optimization_barrier((send(col, CROSS), send(col, SWAP)))
    lead = lead[1](given)
    ahead, behind = send(here, torus(dy=1)), send(here, torus(dy=-1))
    behind, ahead, lead = lax.optimization_barrier((behind, ahead, lead))
    high, low = lax.optimization_barrier(
        (send(behind[128:], torus(dy=-1)), send(ahead[:128], torus(dy=1)))
    )
    far = low, high
    coarse = [here, ahead, behind, *far]
    return coarse + [send(v, SWAP) for v in coarse] + [above, own, below, beside, across], lead


def near_rows(own, rim):
    above, below = send(rim, plane(1, 0)), send(rim, plane(-1, 0))
    col = jnp.concatenate([above, rim, below], axis=0)
    across, beside = lax.optimization_barrier((send(col, CROSS), send(col, SWAP)))
    return above, own, below, beside, across


def shards(
    grid_state,
    mesh_state,
    g2m_features,
    g2m_sender,
    g2m_receiver,
    g2m_blocks,
    proc_features,
    proc_sender,
    proc_receiver,
    dec_features,
    dec_sender,
    enc_weights,
    proc_weights,
    dec_weights,
):
    cells = grid_state.reshape(1024, D)
    nodes = mesh_state.reshape(256, D)
    top = send(grid_state[2:4], plane(1, 0))
    bottom = send(grid_state[0:2], plane(-1, 0))
    grid_send, grid_next, live = grid_kernel(g2m_blocks, cells, enc_weights)
    bottom, top, grid_send = lax.optimization_barrier((bottom, top, grid_send))
    first = jnp.concatenate([top[:, :2], grid_state[:, :2], bottom[:, :2]], axis=0)
    final = jnp.concatenate([top[:, 254:], grid_state[:, 254:], bottom[:, 254:]], axis=0)
    west = send(final.reshape(16, D), plane(0, 1))
    east = send(first.reshape(16, D), plane(0, -1))

    mesh_next, proc_send, proc_recv, both, rim, coarse = enc_kernel(
        live, g2m_sender, g2m_receiver, g2m_features.reshape(-1, D),
        grid_send, top.reshape(512, D), bottom.reshape(512, D), west, east, nodes,
        enc_weights, proc_weights,
    )
    pieces, (lead, self_part) = mesh_rows(
        proc_send, both, rim, coarse, (grid_next, lambda g: lead_kernel(dec_features, g, dec_weights))
    )
    dec_send, rim = proc_kernel(
        proc_features.reshape(-1, D), proc_sender, proc_receiver, pieces, proc_recv,
        mesh_next, proc_weights, dec_weights,
    )
    out = dec_kernel(
        lead, dec_sender, near_rows(dec_send, rim), grid_next, self_part, dec_weights
    )
    return out.reshape(grid_state.shape)


def solution(mesh):
    placed = (
        P("band", "patch", None),
        P("band", "patch", None, None),
        P("band", "patch", None, None),
        P("band", "patch", None),
        P("band", "patch", None),
        P(),
        P("band", "patch", None, None),
        P("band", "patch", None),
        P("band", "patch", None),
        P(None, "band", "patch", None),
        P(None, "band", "patch"),
        P(),
        P(),
        P(),
    )
    return jax.shard_map(
        shards, mesh=mesh, in_specs=placed, out_specs=P("band", "patch", None), check_vma=False
    )
```
